32 devices in a mesh: groups: 2 (over y), ctx: 4 (over x, core), head: 4 (over z).
Axes of the slice: x: 2, y: 2, z: 4, core: 2. Of those that a mesh axis runs over, the one named last changes fastest.
Arguments:
- queries: bfloat16 [1024, 12288], P(('groups', 'ctx'), 'head'), parts along dimension 0, may hold values from -8 to 8
- latent: bfloat16 [65536, 576], P(('groups', 'ctx')), parts along dimension 0, may hold values from -8 to 8
- selection: int32 [8, 64], P(('groups', 'ctx')), parts along dimension 0, may hold values from 0 to 511, as said below
- span_offset: int32 [2], P('groups'), parts along dimension 0, may hold values from 24576 to 32256, as said below
- w_absorb: bfloat16 [64, 128, 512], P('head'), may hold values from -0.5 to 0.5
- w_value: bfloat16 [64, 512, 128], P('head'), may hold values from -4 to 4
- w_out: bfloat16 [8192, 7168], P('head', 'ctx'), may hold values from -0.0625 to 0.0625
Outputs:
- attention_out: bfloat16 [1024, 7168], P(('groups', 'head'), 'ctx'), parts along dimension 0
The draws below stay inside these ranges and needn't reach their ends.
There are 2 independent parts, one for each index of `groups`. The reference program is written for one: setup_inputs(seed, part) draws one part's arguments, and reference() takes and returns one part's arrays. A program takes and returns all parts, laid end to end along the dimension named above; an argument that names none is the same for every part. Nothing has to cross between parts.
Inputs may be any that keep to these rules, and one draw needn't show every extreme that they name: `selection`: row q lists 64 distinct latent blocks, among them block 0. Blocks j * 128 to (j + 1) * 128 - 1 lie on index j of ctx; at most 24 blocks of a row lie on one index, and some index holds exactly 24 blocks of every row. `span_offset`: A multiple of 64.
All inputs are finite; a program needn't handle non-finite values.
Results may differ from the reference program's by a relative error of at most 0.015.
Values may be sent and summed in bfloat16 or wider, within the bound.
No kernel may reach another device: no remote copies, remote signals or barrier semaphores. Data moves between devices by JAX's collectives and lax.ppermute only.
A program may use at most 192 MiB of HBM per device.

```python
import jax
import jax.numpy as jnp
from jax import lax

D = 7168
HEADS = 64
NOPE = 128
ROPE = 64
LAT = 512
VD = 128
BT = 64
TOPK = 64
QB = 128
N_BLK = 512
BLK_DEV = 128
CAP = 24
QTOK = 512
N_CTX = 4
N_HEAD = 4


def span_start(key, part):
    start_key = jax.random.fold_in(key, 101)
    first_block = jax.random.randint(start_key, (), 3 * N_BLK // 4, N_BLK - QTOK // BT + 1)
    return (first_block * BT).astype(jnp.int32)


def draw_span_offset(key, part):
    return span_start(key, part).reshape(1)


def draw_selection(key, part):
    start = span_start(key, part)
    key = jax.random.fold_in(key, 7)
    first_block = start // BT
    full_owner = first_block // BLK_DEV - 1
    blocks_each = QB // BT
    query_block = jnp.arange(N_CTX)[:, None]
    last_block = first_block + (query_block + 1) * blocks_each - 1
    diag_block = first_block + query_block * blocks_each
    block_ids = jnp.arange(N_BLK)[None, :]
    random_part = jax.random.randint(key, (N_CTX, N_BLK), 0, 4096)
    priority = random_part * 4096 + block_ids
    priority = priority + jnp.where(block_ids // BLK_DEV == full_owner, 2 ** 25, 0)
    priority = priority + jnp.where((block_ids >= diag_block) & (block_ids <= last_block), 2 ** 26, 0)
    priority = priority + jnp.where(block_ids == 0, 2 ** 27, 0)
    priority = jnp.where(block_ids <= last_block, priority, block_ids - 2 ** 29)
    grouped = priority.reshape(N_CTX, N_CTX, BLK_DEV)
    ranking = jnp.argsort(-grouped, axis=-1, stable=True)
    standing = jnp.argsort(ranking, axis=-1, stable=True).reshape(N_CTX, N_BLK)
    priority = jnp.where(standing >= CAP, priority - 2 ** 28, priority)
    return lax.top_k(priority, TOPK)[1].astype(jnp.int32)


def draw_latent(key, part):
    key = jax.random.fold_in(key, 5)
    shape = (N_BLK * BT, LAT + ROPE)
    values = jnp.clip(jax.random.normal(key, shape), -4.0, 4.0)
    return values.astype(jnp.bfloat16)


def draw_queries(key, part):
    key = jax.random.fold_in(key, 9)
    shape = (QTOK, HEADS, NOPE + ROPE)
    values = jnp.clip(jax.random.normal(key, shape), -4.0, 4.0)
    return values.reshape(QTOK, HEADS * (NOPE + ROPE)).astype(jnp.bfloat16)


def block_levels(key, shape, shards, low, largest):
    gain = 1.0
    for dim, shards_of in shards:
        heights = jax.random.uniform(jax.random.fold_in(jax.random.fold_in(key, 6), dim), (shards_of,), jnp.float32, low / len(shards), largest / len(shards))
        gain = gain * jnp.repeat(jnp.exp(heights), shape[dim] // shards_of).reshape((-1,) + (1,) * (len(shape) - 1 - dim))
    return gain


def normal_values(own_key, extent, scale, limit, shards=(), kind=jnp.bfloat16):
    drawn = jax.random.normal(own_key, extent, jnp.float32) * scale
    if len(shards) > 0:
        drawn = block_levels(own_key, extent, shards, -0.22, 0.18) * drawn
    return jnp.clip(drawn, min=-limit, max=limit).astype(kind)


def setup_inputs(seed: int = 0, part: int = 0) -> dict:
    key_list = jax.random.split(jax.random.key(seed), 8)
    part_splits = jax.random.split(jax.random.fold_in(key_list[7], part), 8)
    return {
        "queries": draw_queries(jax.random.fold_in(jax.random.fold_in(key_list[7], part), 71), part),
        "latent": draw_latent(jax.random.fold_in(jax.random.fold_in(key_list[7], part), 71), part),
        "selection": draw_selection(jax.random.fold_in(jax.random.fold_in(key_list[7], part), 71), part),
        "span_offset": draw_span_offset(jax.random.fold_in(jax.random.fold_in(key_list[7], part), 71), part),
        "w_absorb": normal_values(key_list[4], (HEADS, NOPE, LAT), NOPE ** -0.5, 0.5, ((0, 4),)),
        "w_value": normal_values(key_list[5], (HEADS, LAT, VD), 2 ** -0.5, 4.0, ((0, 4),)),
        "w_out": normal_values(key_list[6], (HEADS * VD, D), (HEADS * VD) ** -0.5, 0.0625, ((0, 4), (1, 4))),
    }


def reference(queries, latent, selection, span_offset, w_absorb, w_value, w_out):
    row_width = LAT + ROPE
    softmax_scale = (NOPE + ROPE) ** -0.5
    stored = latent.reshape(N_BLK, BT, row_width)
    grouped = queries.reshape(N_CTX, QB, HEADS, NOPE + ROPE)

    def one_block(inputs):
        block_query, chosen_blocks, block_index = inputs
        key_rows = stored[chosen_blocks].reshape(TOPK * BT, row_width)
        key_position = (chosen_blocks[:, None] * BT + jnp.arange(BT, dtype=jnp.int32)[None, :]).reshape(-1)
        query_position = span_offset[0] + block_index * QB + jnp.arange(QB, dtype=jnp.int32)
        visible = key_position[None, :] <= query_position[:, None]
        q_latent = jnp.einsum("qhd,hdl->hql", block_query[:, :, :NOPE].astype(jnp.float32), w_absorb.astype(jnp.float32)).astype(jnp.bfloat16)
        q_full = jnp.concatenate([q_latent, jnp.transpose(block_query[:, :, NOPE:], (1, 0, 2))], axis=2)
        scores = jnp.einsum("hqc,kc->hqk", q_full.astype(jnp.float32), key_rows.astype(jnp.float32)) * softmax_scale
        scores = jnp.where(visible[None, :, :], scores, -jnp.inf)
        row_peak = jnp.max(scores, axis=-1, keepdims=True)
        shifted = jnp.exp(scores - row_peak)
        weights = (shifted / jnp.sum(shifted, axis=-1, keepdims=True)).astype(jnp.bfloat16)
        mixed_latent = jnp.einsum("hqk,kl->hql", weights.astype(jnp.float32), key_rows[:, :LAT].astype(jnp.float32)).astype(jnp.bfloat16)
        head_out = jnp.einsum("hql,hlv->qhv", mixed_latent.astype(jnp.float32), w_value.astype(jnp.float32)).astype(jnp.bfloat16)
        return head_out.reshape(QB, HEADS * VD)

    outputs = lax.map(one_block, (grouped, selection, jnp.arange(N_CTX, dtype=jnp.int32)))
    head_out = outputs.reshape(QTOK, HEADS * VD)
    group_rows = HEADS * VD // N_HEAD

    def add_group(running, group):
        columns = lax.dynamic_slice_in_dim(head_out, group * group_rows, group_rows, 1)
        weight_rows = lax.dynamic_slice_in_dim(w_out, group * group_rows, group_rows, 0)
        partial_value = jnp.dot(columns, weight_rows, preferred_element_type=jnp.float32)
        partial_value = lax.optimization_barrier(partial_value.astype(jnp.bfloat16)).astype(jnp.float32)
        return running + partial_value, None

    summed, _ = lax.scan(add_group, jnp.zeros((QTOK, D), jnp.float32), jnp.arange(N_HEAD, dtype=jnp.int32))
    return summed.astype(jnp.bfloat16)
```

```python
import functools
import math

import jax
import jax.numpy as jnp
from jax import lax
from jax.experimental import pallas as pl
from jax.experimental.pallas import tpu as pltpu
from jax.sharding import PartitionSpec as P

BT = 64
CHUNK = 8
ROW_TILE = 512
NEVER = -1e30
FAR = 1 << 30


def attend_kernel(
    blocks_held, depth, sources, offset,
    meta, q_ref, wa_hbm, own_hbm, sib_hbm, wv_hbm, o_ref,
    kv, q_full, wa, wv, acc, place, edge, kv_sem, wa_sem, wv_sem,
):
    tokens = q_ref.shape[0]
    heads, nope, lat = wa.shape
    width = kv.shape[1]
    vd = wv.shape[2]
    head_width = nope + width - lat
    slots = kv.shape[0] // BT
    step = CHUNK * BT
    fold = head_width ** -0.5 * math.log2(math.e)
    first = meta[64] + offset
    mine = meta[65]
    other = meta[66]

    wa_copy = pltpu.make_async_copy(wa_hbm, wa, wa_sem)
    wv_copy = pltpu.make_async_copy(wv_hbm, wv, wv_sem)
    wa_copy.start()

    def fetch(block, slot):
        owner = block // blocks_held
        row = pl.multiple_of((block % blocks_held) * BT, BT)
        target = kv.at[pl.ds(pl.multiple_of(slot * BT, BT), BT), :]
        if "own" in sources:
            @pl.when(owner == mine)
            def _():
                pltpu.make_async_copy(own_hbm.at[pl.ds(row, BT), :], target, kv_sem).start()
        if "sib" in sources:
            @pl.when(owner == other)
            def _():
                pltpu.make_async_copy(sib_hbm.at[pl.ds(row, BT), :], target, kv_sem).start()

    def scan(j, carry):
        full, part = carry
        block = meta[j]
        owner = block // blocks_held
        here = jnp.bool_(False)
        if "own" in sources:
            here = here | (owner == mine)
        if "sib" in sources:
            here = here | (owner == other)
        whole = here & (block * BT + BT - 1 <= first)
        some = here & (block * BT + BT - 1 > first) & (block * BT <= first + tokens - 1)

        @pl.when(whole)
        def _():
            fetch(block, full)

        @pl.when(some)
        def _():
            edge[part] = block

        return full + whole.astype(jnp.int32), part + some.astype(jnp.int32)

    full, part = lax.fori_loop(0, 64, scan, (jnp.int32(0), jnp.int32(0)))

    def fetch_edge(i, _):
        fetch(edge[i], full + i)
        place[full + i] = edge[i] * BT
        return 0

    lax.fori_loop(0, part, fetch_edge, 0)
    count = full + part
    chunks = jnp.maximum((count + CHUNK - 1) // CHUNK, 1)

    def fill(i, _):
        target = kv.at[pl.ds(pl.multiple_of(i * BT, BT), BT), :]
        pltpu.make_async_copy(own_hbm.at[pl.ds(0, BT), :], target, kv_sem).start()
        place[i] = FAR
        return 0

    lax.fori_loop(count, chunks * CHUNK, fill, 0)
    plain = full // CHUNK

    def clear(i, _):
        place[i] = 0
        return 0

    lax.fori_loop(plain * CHUNK, full, clear, 0)
    wv_copy.start()

    wa_copy.wait()
    for h in range(heads):
        base = h * head_width
        latent_part = jnp.dot(
            q_ref[:, base : base + nope], wa[h], preferred_element_type=jnp.float32
        )
        rows = slice(h * tokens, (h + 1) * tokens)
        q_full[rows, 0:lat] = (latent_part * fold).astype(jnp.bfloat16)
        turned = q_ref[:, base + nope : base + head_width].astype(jnp.float32)
        q_full[rows, lat:width] = (turned * fold).astype(jnp.bfloat16)

    def land(i, _):
        pltpu.make_async_copy(own_hbm.at[pl.ds(0, BT), :], kv.at[pl.ds(0, BT), :], kv_sem).wait()
        return 0

    lax.fori_loop(0, chunks * CHUNK, land, 0)
    wv_copy.wait()

    tile = min(ROW_TILE, heads * tokens)
    tile_heads = tile // tokens
    lane = lax.broadcasted_iota(jnp.int32, (tokens, 128), 1)

    def row_tile(r, lse_tile):
        row0 = pl.multiple_of(r * tile, tile)
        acc[...] = jnp.zeros_like(acc)

        def chunk(masked, c, carry):
            peak, total = carry
            keys = pl.ds(pl.multiple_of(c * step, step), step)
            scores = lax.dot_general(
                q_full[pl.ds(row0, tile), :], kv[keys, :], (((1,), (1,)), ((), ())),
                preferred_element_type=jnp.float32,
            )
            if masked:
                column = lax.broadcasted_iota(jnp.int32, (tokens, step), 1)
                position = jnp.zeros((tokens, step), jnp.int32)
                for b in range(CHUNK):
                    position = jnp.where(
                        column // BT == b, place[c * CHUNK + b] + column % BT, position
                    )
                query = first + lax.broadcasted_iota(jnp.int32, (tokens, step), 0)
                visible = position <= query
                scores = jnp.where(
                    visible[None], scores.reshape(tile_heads, tokens, step), NEVER
                ).reshape(tile, step)
            new_peak = jnp.maximum(peak, jnp.max(scores, axis=1, keepdims=True))
            raised = jnp.exp2(scores - new_peak)
            keep = jnp.exp2(peak - new_peak)
            total = total * keep
            for n in range(step // 128):
                total = total + raised[:, n * 128 : (n + 1) * 128]
            acc[...] = acc[...] * keep + jnp.dot(
                raised.astype(jnp.bfloat16), kv[keys, 0:lat], preferred_element_type=jnp.float32
            )
            return new_peak, total

        carry = (jnp.full((tile, 1), NEVER, jnp.float32), jnp.zeros((tile, 128), jnp.float32))
        carry = lax.fori_loop(0, plain, functools.partial(chunk, False), carry)
        peak, total = lax.fori_loop(plain, chunks, functools.partial(chunk, True), carry)
        total = jnp.sum(total, axis=1, keepdims=True)
        lse = peak + jnp.log2(total)
        scale = 1.0 / total
        for i in range(tile_heads):
            h = r * tile_heads + i
            rows = slice(i * tokens, (i + 1) * tokens)
            mixed = (acc[rows, :] * scale[rows, :]).astype(jnp.bfloat16)
            out = jnp.dot(mixed, wv[h], preferred_element_type=jnp.float32)
            o_ref[:, pl.ds(pl.multiple_of(h * vd, vd), vd)] = out.astype(jnp.bfloat16)
            value = lse[rows, :]
            high = value.astype(jnp.bfloat16).astype(jnp.float32)
            middle = (value - high).astype(jnp.bfloat16).astype(jnp.float32)
            low = value - high - middle
            lse_tile = jnp.where(lane == h, high, lse_tile)
            lse_tile = jnp.where(lane == h + 32, middle, lse_tile)
            lse_tile = jnp.where(lane == h + 64, low, lse_tile)
        return lse_tile

    lse_tile = lax.fori_loop(
        0, heads * tokens // tile, row_tile, jnp.zeros((tokens, 128), jnp.float32)
    )
    o_ref[:, heads * vd :] = lse_tile.astype(jnp.bfloat16)


def attend(meta, queries, own, sib, w_absorb, w_value, depth, sources, offset=0):
    tokens = queries.shape[0]
    heads, nope, lat = w_absorb.shape
    vd = w_value.shape[2]
    width = own.shape[1]
    slots = -(-depth * len(sources) // CHUNK) * CHUNK
    rows = heads * tokens
    tile = min(ROW_TILE, rows)
    keys = depth * len(sources) * BT * 2 // 3
    any_space = pl.BlockSpec(memory_space=pl.ANY)
    vmem = pl.BlockSpec(memory_space=pltpu.VMEM)
    return pl.pallas_call(
        functools.partial(attend_kernel, own.shape[0] // BT, depth, sources, offset),
        out_shape=jax.ShapeDtypeStruct((tokens, heads * vd + 128), jnp.bfloat16),
        in_specs=[
            pl.BlockSpec(memory_space=pltpu.SMEM), vmem, any_space, any_space, any_space, any_space,
        ],
        out_specs=vmem,
        scratch_shapes=[
            pltpu.VMEM((slots * BT, width), jnp.bfloat16),
            pltpu.VMEM((rows, width), jnp.bfloat16),
            pltpu.VMEM(w_absorb.shape, jnp.bfloat16),
            pltpu.VMEM(w_value.shape, jnp.bfloat16),
            pltpu.VMEM((tile, lat), jnp.float32),
            pltpu.SMEM((slots,), jnp.int32),
            pltpu.SMEM((64,), jnp.int32),
            pltpu.SemaphoreType.DMA,
            pltpu.SemaphoreType.DMA,
            pltpu.SemaphoreType.DMA,
        ],
        compiler_params=pltpu.CompilerParams(vmem_limit_bytes=40 * 1024 * 1024),
        cost_estimate=pl.CostEstimate(
            flops=2 * rows * keys * (width + lat),
            bytes_accessed=2 * keys * width * 2,
            transcendentals=rows * keys,
        ),
    )(meta, queries, w_absorb, own, sib, w_value)


def split_partial(partial, heads):
    values = partial[:, :-128].astype(jnp.float32).reshape(partial.shape[0], heads, -1)
    tail = partial[:, -128:].astype(jnp.float32)
    lse = tail[:, 0:heads] + tail[:, 32 : 32 + heads] + tail[:, 64 : 64 + heads]
    return values, lse


def combine(partials, heads):
    parts = [split_partial(p, heads) for p in partials]
    peak = functools.reduce(jnp.maximum, [lse for _, lse in parts])
    shares = [jnp.exp2(lse - peak) for _, lse in parts]
    norm = 1.0 / functools.reduce(jnp.add, shares)
    mixed = sum(v * (s * norm)[:, :, None] for (v, _), s in zip(parts, shares))
    return mixed.reshape(mixed.shape[0], -1).astype(jnp.bfloat16)


def body(queries, latent, selection, span_offset, w_absorb, w_value, w_out):
    owners = lax.axis_size("ctx")
    me = lax.axis_index("ctx")
    chips = owners // 2
    depth = 3 * selection.shape[1] // (2 * owners)
    heads = w_absorb.shape[0]
    tokens = queries.shape[0]
    sibling = [(i, i ^ 1) for i in range(owners)]
    sib_latent = lax.ppermute(latent, "ctx", sibling)

    def meta_of(row, index):
        return jnp.concatenate(
            [row[0], jnp.stack([span_offset[0] + index * tokens, me, me ^ 1])]
        ).astype(jnp.int32)

    own_partials = [
        attend(meta_of(selection, me), queries, latent, latent, w_absorb, w_value, depth, ("own",)),
        attend(meta_of(selection, me), queries, latent, sib_latent, w_absorb, w_value, depth, ("sib",)),
    ]
    for turn in range(1, chips):
        ahead = [(i, (i + 2 * turn) % owners) for i in range(owners)]
        back = [(i, (i - 2 * turn) % owners) for i in range(owners)]
        far_queries = lax.ppermute(queries, "ctx", ahead)
        far_rows = lax.ppermute(selection, "ctx", ahead)
        index = (me - 2 * turn) % owners
        partial = attend(
            meta_of(far_rows, index), far_queries, latent, sib_latent, w_absorb, w_value, depth, ("own", "sib")
        )
        own_partials.append(lax.ppermute(partial, "ctx", back))
    head_out = combine(own_partials, heads)
    gathered = lax.all_gather(head_out, "ctx", axis=0, tiled=True)
    return lax.psum_scatter(
        jnp.dot(gathered, w_out, preferred_element_type=jnp.float32).astype(jnp.bfloat16),
        "head",
        scatter_dimension=0,
        tiled=True,
    )


def solution(mesh):
    placed = (
        P(("groups", "ctx"), "head"),
        P(("groups", "ctx"), None),
        P(("groups", "ctx"), None),
        P("groups"),
        P("head", None, None),
        P("head", None, None),
        P("head", "ctx"),
    )
    return jax.shard_map(
        body, mesh=mesh, in_specs=placed, out_specs=P(("groups", "head"), "ctx"), check_vma=False
    )
```

```python
import functools
import math

import jax
import jax.numpy as jnp
from jax import lax
from jax.experimental import pallas as pl
from jax.experimental.pallas import tpu as pltpu
from jax.sharding import PartitionSpec as P

BT = 64
WIDE = 128
CHUNK = 8
SMALL = 4
PIECES = 2
NEVER = -1e30
FAR = 1 << 30
MIB = 1024 * 1024


def attend_kernel(
    blocks_held, sources, offset,
    meta, q_ref, wa_hbm, own_hbm, sib_hbm, wv_hbm, o_ref,
    raw, kt, q_full, wa, wv, acc0, acc1, s0, s1, p0, p1, t0, t1, listed, edge, kv_sem, wa_sem, wv_sem,
):
    accs, stores, peaks, totals = (acc0, acc1), (s0, s1), (p0, p1), (t0, t1)
    tokens = q_ref.shape[0]
    heads, nope, lat = wa.shape
    width = kt.shape[0]
    vd = wv.shape[2]
    head_width = nope + width - lat
    fold = head_width ** -0.5 * math.log2(math.e)
    first = meta[64] + offset
    mine = meta[65]
    other = meta[66]

    wa_copy = pltpu.make_async_copy(wa_hbm, wa, wa_sem)
    wv_copy = pltpu.make_async_copy(wv_hbm, wv, wv_sem)
    wa_copy.start()

    def fetch(block, slot):
        owner = block // blocks_held
        col = pl.multiple_of((block % blocks_held) // 2 * WIDE, WIDE)
        for name, holder, source in (("own", mine, own_hbm), ("sib", other, sib_hbm)):
            if name in sources:
                @pl.when(owner == holder)
                def _(source=source):
                    pltpu.make_async_copy(source.at[:, pl.ds(col, WIDE)], raw.at[slot], kv_sem).start()

    def scan(j, carry):
        full, part = carry
        block = meta[j]
        owner = block // blocks_held
        here = jnp.bool_(False)
        for name, holder in (("own", mine), ("sib", other)):
            if name in sources:
                here = here | (owner == holder)
        whole = here & (block * BT + BT - 1 <= first)
        some = here & (block * BT + BT - 1 > first) & (block * BT <= first + tokens - 1)

        @pl.when(whole)
        def _():
            fetch(block, full)
            listed[full] = block

        @pl.when(some)
        def _():
            edge[part] = block

        return full + whole.astype(jnp.int32), part + some.astype(jnp.int32)

    full, part = lax.fori_loop(0, 64, scan, (jnp.int32(0), jnp.int32(0)))

    def fetch_edge(i, _):
        fetch(edge[i], full + i)
        listed[full + i] = edge[i]
        return 0

    lax.fori_loop(0, part, fetch_edge, 0)
    count = full + part
    plain_chunks = full // CHUNK
    done = plain_chunks * CHUNK
    small_chunks = (count - done + SMALL - 1) // SMALL
    slots = done + small_chunks * SMALL

    def fill(i, _):
        pltpu.make_async_copy(own_hbm.at[:, pl.ds(0, WIDE)], raw.at[i], kv_sem).start()
        listed[i] = 0
        return 0

    lax.fori_loop(count, slots, fill, 0)
    wv_copy.start()

    wa_copy.wait()
    for h in range(heads):
        base = h * head_width
        latent_part = jnp.dot(
            q_ref[:, base : base + nope], wa[h], preferred_element_type=jnp.float32
        )
        rows = slice(h * tokens, (h + 1) * tokens)
        q_full[rows, 0:lat] = (latent_part * fold).astype(jnp.bfloat16)
        turned = q_ref[:, base + nope : base + head_width].astype(jnp.float32)
        q_full[rows, lat:width] = (turned * fold).astype(jnp.bfloat16)

    def land(i, _):
        pltpu.make_async_copy(own_hbm.at[:, pl.ds(0, WIDE)], raw.at[0], kv_sem).wait()
        return 0

    lax.fori_loop(0, slots, land, 0)

    def join(i, _):
        left = raw[2 * i]
        right = raw[2 * i + 1]
        left_swapped = jnp.concatenate([left[:, BT:], left[:, :BT]], axis=1)
        right_swapped = jnp.concatenate([right[:, BT:], right[:, :BT]], axis=1)
        low = jnp.where(listed[2 * i] % 2 == 1, left_swapped, left)
        high = jnp.where(listed[2 * i + 1] % 2 == 1, right, right_swapped)
        lane = lax.broadcasted_iota(jnp.int32, (width, WIDE), 1)
        kt[:, pl.ds(pl.multiple_of(i * WIDE, WIDE), WIDE)] = jnp.where(lane < BT, low, high)
        return 0

    lax.fori_loop(0, slots // 2, join, 0)
    wv_copy.wait()

    tile = acc0.shape[0]
    tile_heads = tile // tokens
    lane = lax.broadcasted_iota(jnp.int32, (tokens, 128), 1)

    def row_pair(r, lse_tile):
        bases = [pl.multiple_of(r * 2 * tile, tile), pl.multiple_of(r * 2 * tile + tile, tile)]
        for i in range(2):
            accs[i][...] = jnp.zeros_like(accs[i])
            peaks[i][...] = jnp.full(peaks[i].shape, NEVER, jnp.float32)
            totals[i][...] = jnp.zeros_like(totals[i])

        def score(i, key0, n):
            stores[i][:, 0 : n * BT] = jnp.dot(
                q_full[pl.ds(bases[i], tile), :], kt[:, pl.ds(key0, n * BT)],
                preferred_element_type=jnp.float32,
            )

        def soften(i, n, visible):
            scores = stores[i][:, 0 : n * BT]
            if visible is not None:
                scores = jnp.where(
                    visible[None], scores.reshape(tile_heads, tokens, n * BT), NEVER
                ).reshape(tile, n * BT)
            peak = peaks[i][...]
            new_peak = jnp.maximum(peak, jnp.max(scores, axis=1, keepdims=True))
            peaks[i][...] = new_peak
            raised = jnp.exp2(scores - new_peak[:, 0:1])
            keep = jnp.exp2(peak - new_peak)
            total = totals[i][...] * keep
            for k in range(n * BT // 128):
                total = total + raised[:, k * 128 : (k + 1) * 128]
            totals[i][...] = total
            return raised.astype(jnp.bfloat16), keep[:, 0:1]

        def mix(i, key0, n, raised, keep):
            accs[i][...] = accs[i][...] * keep + lax.dot_general(
                raised, kt[0:lat, pl.ds(key0, n * BT)], (((1,), (1,)), ((), ())),
                preferred_element_type=jnp.float32,
            )

        def chunk(n, total_chunks, start, masked, c, _):
            key0 = pl.multiple_of(start + c * n * BT, 128)
            last = start + (total_chunks - 1) * n * BT
            key1 = pl.multiple_of(jnp.minimum(key0 + n * BT, last), 128)
            visible = None
            if masked:
                block0 = key0 // BT
                column = lax.broadcasted_iota(jnp.int32, (tokens, n * BT), 1)
                position = jnp.zeros((tokens, n * BT), jnp.int32)
                for b in range(n):
                    at = jnp.where(
                        block0 + b < full, 0,
                        jnp.where(block0 + b < count, listed[block0 + b] * BT, FAR),
                    )
                    position = jnp.where(column // BT == b, at + column % BT, position)
                query = first + lax.broadcasted_iota(jnp.int32, (tokens, n * BT), 0)
                visible = position <= query
            score(1, key0, n)
            raised, keep = soften(0, n, visible)
            mix(0, key0, n, raised, keep)
            score(0, key1, n)
            raised, keep = soften(1, n, visible)
            mix(1, key0, n, raised, keep)
            return 0

        @pl.when(plain_chunks > 0)
        def _():
            score(0, 0, CHUNK)
            lax.fori_loop(
                0, plain_chunks, functools.partial(chunk, CHUNK, plain_chunks, 0, False), 0
            )

        @pl.when(small_chunks > 0)
        def _():
            score(0, pl.multiple_of(done * BT, 128), SMALL)
            lax.fori_loop(
                0, small_chunks, functools.partial(chunk, SMALL, small_chunks, done * BT, True), 0
            )

        for i in range(2):
            total = jnp.maximum(jnp.sum(totals[i][...], axis=1, keepdims=True), 1e-30)
            lse = peaks[i][:, 0:1] + jnp.log2(total)
            scale = 1.0 / total
            for j in range(tile_heads):
                h = (r * 2 + i) * tile_heads + j
                rows = slice(j * tokens, (j + 1) * tokens)
                mixed = (accs[i][rows, :] * scale[rows, :]).astype(jnp.bfloat16)
                out = jnp.dot(mixed, wv[h], preferred_element_type=jnp.float32)
                o_ref[:, pl.ds(pl.multiple_of(h * vd, vd), vd)] = out.astype(jnp.bfloat16)
                value = lse[rows, :]
                high = value.astype(jnp.bfloat16).astype(jnp.float32)
                middle = (value - high).astype(jnp.bfloat16).astype(jnp.float32)
                low = value - high - middle
                lse_tile = jnp.where(lane == h, high, lse_tile)
                lse_tile = jnp.where(lane == h + 32, middle, lse_tile)
                lse_tile = jnp.where(lane == h + 64, low, lse_tile)
        return lse_tile

    lse_tile = lax.fori_loop(
        0, heads * tokens // (2 * tile), row_pair, jnp.zeros((tokens, 128), jnp.float32)
    )
    o_ref[:, heads * vd :] = lse_tile.astype(jnp.bfloat16)


def attend(meta, queries, own, sib, w_absorb, w_value, depth, sources, offset, row_tile):
    tokens = queries.shape[0]
    heads, nope, lat = w_absorb.shape
    vd = w_value.shape[2]
    width = own.shape[0]
    slots = -(-depth * len(sources) // SMALL) * SMALL
    rows = heads * tokens
    tile = min(row_tile, rows // 2)
    keys = depth * len(sources) * BT * 2 // 3
    any_space = pl.BlockSpec(memory_space=pl.ANY)
    vmem = pl.BlockSpec(memory_space=pltpu.VMEM)
    return pl.pallas_call(
        functools.partial(attend_kernel, own.shape[1] // BT, sources, offset),
        out_shape=jax.ShapeDtypeStruct((tokens, heads * vd + 128), jnp.bfloat16),
        in_specs=[
            pl.BlockSpec(memory_space=pltpu.SMEM), vmem, any_space, any_space, any_space, any_space,
        ],
        out_specs=vmem,
        scratch_shapes=[
            pltpu.VMEM((slots, width, WIDE), jnp.bfloat16),
            pltpu.VMEM((width, slots * BT), jnp.bfloat16),
            pltpu.VMEM((rows, width), jnp.bfloat16),
            pltpu.VMEM(w_absorb.shape, jnp.bfloat16),
            pltpu.VMEM(w_value.shape, jnp.bfloat16),
            *[pltpu.VMEM((tile, lat), jnp.float32)] * 2,
            *[pltpu.VMEM((tile, CHUNK * BT), jnp.float32)] * 2,
            *[pltpu.VMEM((tile, 128), jnp.float32)] * 4,
            pltpu.SMEM((slots,), jnp.int32),
            pltpu.SMEM((64,), jnp.int32),
            pltpu.SemaphoreType.DMA,
            pltpu.SemaphoreType.DMA,
            pltpu.SemaphoreType.DMA,
        ],
        compiler_params=pltpu.CompilerParams(vmem_limit_bytes=52 * MIB),
        cost_estimate=pl.CostEstimate(
            flops=2 * rows * keys * (width + lat),
            bytes_accessed=2 * keys * width * 2,
            transcendentals=rows * keys,
        ),
    )(meta, queries, w_absorb, own, sib, w_value)


def combine_kernel(heads, *refs):
    partials, out = refs[:-1], refs[-1]
    vd = out.shape[1] // heads
    logs = []
    for ref in partials:
        tail = ref[:, heads * vd :].astype(jnp.float32)
        logs.append(tail[:, 0:heads] + tail[:, 32 : 32 + heads] + tail[:, 64 : 64 + heads])
    peak = functools.reduce(jnp.maximum, logs)
    shares = [jnp.exp2(value - peak) for value in logs]
    norm = 1.0 / functools.reduce(jnp.add, shares)
    for h in range(heads):
        columns = slice(h * vd, (h + 1) * vd)
        mixed = sum(
            ref[:, columns].astype(jnp.float32) * (share * norm)[:, h : h + 1]
            for ref, share in zip(partials, shares)
        )
        out[:, columns] = mixed.astype(jnp.bfloat16)


def combine(partials, heads):
    tokens, columns = partials[0].shape
    vmem = pl.BlockSpec(memory_space=pltpu.VMEM)
    return pl.pallas_call(
        functools.partial(combine_kernel, heads),
        out_shape=jax.ShapeDtypeStruct((tokens, columns - 128), jnp.bfloat16),
        in_specs=[vmem] * len(partials),
        out_specs=vmem,
        compiler_params=pltpu.CompilerParams(vmem_limit_bytes=16 * MIB),
        cost_estimate=pl.CostEstimate(
            flops=4 * tokens * columns, bytes_accessed=8 * tokens * columns, transcendentals=0
        ),
    )(*partials)


def project_kernel(x_ref, w_ref, o_ref):
    o_ref[...] = jnp.dot(x_ref[...], w_ref[...], preferred_element_type=jnp.float32).astype(jnp.bfloat16)


def project(x, w):
    rows, depth = x.shape
    columns = w.shape[1]
    wide = 256 if columns % 256 == 0 else columns
    return pl.pallas_call(
        project_kernel,
        out_shape=jax.ShapeDtypeStruct((rows, columns), jnp.bfloat16),
        grid=(columns // wide,),
        in_specs=[
            pl.BlockSpec((rows, depth), lambda j: (0, 0)),
            pl.BlockSpec((depth, wide), lambda j: (0, j)),
        ],
        out_specs=pl.BlockSpec((rows, wide), lambda j: (0, j)),
        compiler_params=pltpu.CompilerParams(vmem_limit_bytes=32 * MIB),
        cost_estimate=pl.CostEstimate(
            flops=2 * rows * depth * columns,
            bytes_accessed=2 * (rows * depth + depth * columns + rows * columns),
            transcendentals=0,
        ),
    )(x, w)


def body(queries, latent, selection, span_offset, w_absorb, w_value, w_out):
    owners = lax.axis_size("ctx")
    groups = lax.axis_size("head")
    me = lax.axis_index("ctx")
    column = lax.axis_index("head")
    chips = owners // 2
    depth = 3 * selection.shape[1] // (2 * owners)
    heads = w_absorb.shape[0]
    tokens = queries.shape[0]
    piece = tokens // PIECES
    sibling = [(i, i ^ 1) for i in range(owners)]
    ahead = {t: [(i, (i + 2 * t) % owners) for i in range(owners)] for t in range(1, chips)}
    back = {t: [(i, (i - 2 * t) % owners) for i in range(owners)] for t in range(1, chips)}
    own = latent.T

    def meta_of(row, index):
        return jnp.concatenate(
            [row[0], jnp.stack([span_offset[0] + index * tokens, me, me ^ 1])]
        ).astype(jnp.int32)

    cuts = [slice(c * piece, (c + 1) * piece) for c in range(PIECES)]
    far_rows = {t: lax.ppermute(selection, "ctx", ahead[t]) for t in ahead}
    far_queries = [
        {t: lax.ppermute(queries[cut], "ctx", ahead[t]) for t in ahead} for cut in cuts
    ]
    sib = lax.ppermute(own, "ctx", sibling)
    my_meta = meta_of(selection, me)
    near = attend(my_meta, queries, own, own, w_absorb, w_value, depth, ("own",), 0, 1024)
    outputs = []
    for c, cut in enumerate(cuts):
        partials = []
        for t in ahead:
            partial = attend(
                meta_of(far_rows[t], (me - 2 * t) % owners), far_queries[c][t], own, sib,
                w_absorb, w_value, depth, ("own", "sib"), c * piece, 512,
            )
            partials.append(lax.ppermute(partial, "ctx", back[t]))
        partials.append(
            attend(my_meta, queries[cut], own, sib, w_absorb, w_value, depth, ("sib",), c * piece, 512)
        )
        partials.append(near[cut])
        mine = combine(partials, heads)
        gathered = [mine] + [lax.ppermute(mine, "ctx", ahead[t]) for t in ahead]
        pairs = [x for g in gathered for x in (g, lax.ppermute(g, "ctx", sibling))]
        shares = project(jnp.concatenate(pairs, axis=0), w_out)

        def share_of(block):
            turn = (me // 2 - block // 2) % chips
            place = turn * 2 + (me + block) % 2
            return lax.dynamic_slice_in_dim(shares, place * piece, piece, 0)

        arrived = [share_of(column)]
        order = sorted(range(1, groups), key=lambda s: -min(s, groups - s))
        for s in order:
            shift = [(i, (i + s) % groups) for i in range(groups)]
            arrived.append(lax.ppermute(share_of((column + s) % groups), "head", shift))
        outputs.append(sum(a.astype(jnp.float32) for a in arrived).astype(jnp.bfloat16))
    return jnp.concatenate(outputs, axis=0)


def solution(mesh):
    placed = (
        P(("groups", "ctx"), "head"),
        P(("groups", "ctx"), None),
        P(("groups", "ctx"), None),
        P("groups"),
        P("head", None, None),
        P("head", None, None),
        P("head", "ctx"),
    )
    return jax.shard_map(
        body, mesh=mesh, in_specs=placed, out_specs=P(("groups", "head"), "ctx"), check_vma=False
    )
```

```python
import functools
import math

import jax
import jax.numpy as jnp
from jax import lax
from jax.experimental import pallas as pl
from jax.experimental.pallas import tpu as pltpu
from jax.sharding import PartitionSpec as P

BT = 64
WIDE = 128
CHUNK = 8
SMALL = 4
PIECES = 2
NEVER = -1e30
FAR = 1 << 30
MIB = 1024 * 1024
META = 67


def attend_kernel(blocks_held, jobs, fresh, keep, *refs):
    refs = list(refs)
    n = len(jobs)

    def take(k):
        out = refs[:k]
        del refs[:k]
        return out

    (meta,) = take(1)
    queries = take(n)
    wa_hbm, own_hbm, sib_hbm, wv_hbm = take(4)
    saved, listed = ([], None) if fresh else (take(n), take(1)[0])
    outs = take(n)
    kept = take(n) if keep else []
    if keep:
        (listed,) = take(1)
    raws = take(n) if fresh else []
    kts = take(n)
    q_full, wa, wv = take(3)
    accs, stores, peaks, totals = take(2), take(2), take(2), take(2)
    if fresh and not keep:
        (listed,) = take(1)
    edge, wa_sem, wv_sem, kv_sems, keep_sems = take(5)

    tokens = queries[0].shape[0]
    heads, nope, lat = wa.shape
    width = kts[0].shape[0]
    vd = wv.shape[2]
    head_width = nope + width - lat
    fold = head_width ** -0.5 * math.log2(math.e)
    strides = [0]
    for kt in kts:
        strides.append(strides[-1] + kt.shape[1] // BT + 2)

    wa_copy = pltpu.make_async_copy(wa_hbm, wa, wa_sem)
    wv_copy = pltpu.make_async_copy(wv_hbm, wv, wv_sem)
    wa_copy.start()

    def gather(j):
        row0, list0 = META * j, strides[j]
        room = kts[j].shape[1] // BT
        start, mine, other = meta[row0 + 64], meta[row0 + 65], meta[row0 + 66]
        raw, sem = raws[j], kv_sems.at[j]
        holders = [
            h for h in (("own", mine, own_hbm), ("sib", other, sib_hbm)) if h[0] in jobs[j][0]
        ]

        def fetch(block, slot):
            owner = block // blocks_held
            col = pl.multiple_of((block % blocks_held) // 2 * WIDE, WIDE)
            for _, holder, source in holders:
                @pl.when(owner == holder)
                def _(source=source):
                    pltpu.make_async_copy(source.at[:, pl.ds(col, WIDE)], raw.at[slot], sem).start()

        def scan(i, carry):
            full, part = carry
            block = meta[row0 + i]
            owner = block // blocks_held
            here = jnp.bool_(False)
            for _, holder, _ in holders:
                here = here | (owner == holder)
            whole = here & (block * BT + BT - 1 <= start)
            some = here & (block * BT + BT - 1 > start) & (block * BT <= start + jobs[j][1] - 1)

            @pl.when(whole)
            def _():
                fetch(block, full)
                listed[list0 + full] = block

            @pl.when(some)
            def _():
                edge[part] = block

            return full + whole.astype(jnp.int32), part + some.astype(jnp.int32)

        full, part = lax.fori_loop(0, 64, scan, (jnp.int32(0), jnp.int32(0)))

        def fetch_edge(i, _):
            fetch(edge[i], full + i)
            listed[list0 + full + i] = edge[i]
            return 0

        lax.fori_loop(0, part, fetch_edge, 0)
        count = full + part

        def fill(i, _):
            pltpu.make_async_copy(own_hbm.at[:, pl.ds(0, WIDE)], raw.at[i], sem).start()
            listed[list0 + i] = 0
            return 0

        lax.fori_loop(count, (count + SMALL - 1) // SMALL * SMALL, fill, 0)
        listed[list0 + room] = full
        listed[list0 + room + 1] = count

    def join(j):
        raw, kt, list0 = raws[j], kts[j], strides[j]
        count = listed[list0 + kt.shape[1] // BT + 1]
        slots = (count + SMALL - 1) // SMALL * SMALL

        def land(i, _):
            pltpu.make_async_copy(own_hbm.at[:, pl.ds(0, WIDE)], raw.at[0], kv_sems.at[j]).wait()
            return 0

        lax.fori_loop(0, slots, land, 0)

        def pair(i, _):
            left = raw[2 * i]
            right = raw[2 * i + 1]
            left_swapped = jnp.concatenate([left[:, BT:], left[:, :BT]], axis=1)
            right_swapped = jnp.concatenate([right[:, BT:], right[:, :BT]], axis=1)
            low = jnp.where(listed[list0 + 2 * i] % 2 == 1, left_swapped, left)
            high = jnp.where(listed[list0 + 2 * i + 1] % 2 == 1, right, right_swapped)
            lane = lax.broadcasted_iota(jnp.int32, (width, WIDE), 1)
            kt[:, pl.ds(pl.multiple_of(i * WIDE, WIDE), WIDE)] = jnp.where(lane < BT, low, high)
            return 0

        lax.fori_loop(0, slots // 2, pair, 0)

    if fresh:
        for j in range(n):
            gather(j)
    else:
        for j in range(n):
            pltpu.make_async_copy(saved[j], kts[j], kv_sems.at[j]).start()
    wv_copy.start()
    wa_copy.wait()
    rows_each = heads * tokens
    for j in range(n):
        for h in range(heads):
            base = h * head_width
            latent_part = jnp.dot(
                queries[j][:, base : base + nope], wa[h], preferred_element_type=jnp.float32
            )
            rows = slice(j * rows_each + h * tokens, j * rows_each + (h + 1) * tokens)
            q_full[rows, 0:lat] = (latent_part * fold).astype(jnp.bfloat16)
            turned = queries[j][:, base + nope : base + head_width].astype(jnp.float32)
            q_full[rows, lat:width] = (turned * fold).astype(jnp.bfloat16)
    for j in range(n):
        if fresh:
            join(j)
        else:
            pltpu.make_async_copy(saved[j], kts[j], kv_sems.at[j]).wait()
        if keep:
            pltpu.make_async_copy(kts[j], kept[j], keep_sems.at[j]).start()
    wv_copy.wait()

    tile = accs[0].shape[0]
    tile_heads = tile // tokens
    lane = lax.broadcasted_iota(jnp.int32, (tokens, 128), 1)

    def work(j):
        kt, list0, o_ref = kts[j], strides[j], outs[j]
        room = kt.shape[1] // BT
        first = meta[META * j + 64] + jobs[j][2]
        full = listed[list0 + room]
        count = listed[list0 + room + 1]
        plain_chunks = full // CHUNK
        done = plain_chunks * CHUNK
        small_chunks = (count - done + SMALL - 1) // SMALL

        def row_pair(r, lse_tile):
            row0 = j * rows_each + r * 2 * tile
            bases = [pl.multiple_of(row0, tile), pl.multiple_of(row0 + tile, tile)]
            for i in range(2):
                accs[i][...] = jnp.zeros_like(accs[i])
                peaks[i][...] = jnp.full(peaks[i].shape, NEVER, jnp.float32)
                totals[i][...] = jnp.zeros_like(totals[i])

            def score(i, key0, n):
                stores[i][:, 0 : n * BT] = jnp.dot(
                    q_full[pl.ds(bases[i], tile), :], kt[:, pl.ds(key0, n * BT)],
                    preferred_element_type=jnp.float32,
                )

            def soften(i, n, visible):
                scores = stores[i][:, 0 : n * BT]
                if visible is not None:
                    scores = jnp.where(
                        visible[None], scores.reshape(tile_heads, tokens, n * BT), NEVER
                    ).reshape(tile, n * BT)
                peak = peaks[i][...]
                new_peak = jnp.maximum(peak, jnp.max(scores, axis=1, keepdims=True))
                peaks[i][...] = new_peak
                raised = jnp.exp2(scores - new_peak[:, 0:1])
                keep_share = jnp.exp2(peak - new_peak)
                total = totals[i][...] * keep_share
                for k in range(n * BT // 128):
                    total = total + raised[:, k * 128 : (k + 1) * 128]
                totals[i][...] = total
                return raised.astype(jnp.bfloat16), keep_share[:, 0:1]

            def mix(i, key0, n, raised, keep_share):
                accs[i][...] = accs[i][...] * keep_share + lax.dot_general(
                    raised, kt[0:lat, pl.ds(key0, n * BT)], (((1,), (1,)), ((), ())),
                    preferred_element_type=jnp.float32,
                )

            def chunk(n, total_chunks, start, masked, c, _):
                key0 = pl.multiple_of(start + c * n * BT, 128)
                last = start + (total_chunks - 1) * n * BT
                key1 = pl.multiple_of(jnp.minimum(key0 + n * BT, last), 128)
                visible = None
                if masked:
                    block0 = key0 // BT
                    column = lax.broadcasted_iota(jnp.int32, (tokens, n * BT), 1)
                    position = jnp.zeros((tokens, n * BT), jnp.int32)
                    for b in range(n):
                        at = jnp.where(
                            block0 + b < full, 0,
                            jnp.where(block0 + b < count, listed[list0 + block0 + b] * BT, FAR),
                        )
                        position = jnp.where(column // BT == b, at + column % BT, position)
                    query = first + lax.broadcasted_iota(jnp.int32, (tokens, n * BT), 0)
                    visible = position <= query
                score(1, key0, n)
                raised, share = soften(0, n, visible)
                mix(0, key0, n, raised, share)
                score(0, key1, n)
                raised, share = soften(1, n, visible)
                mix(1, key0, n, raised, share)
                return 0

            @pl.when(plain_chunks > 0)
            def _():
                score(0, 0, CHUNK)
                lax.fori_loop(
                    0, plain_chunks, functools.partial(chunk, CHUNK, plain_chunks, 0, False), 0
                )

            @pl.when(small_chunks > 0)
            def _():
                score(0, pl.multiple_of(done * BT, 128), SMALL)
                lax.fori_loop(
                    0, small_chunks, functools.partial(chunk, SMALL, small_chunks, done * BT, True), 0
                )

            for i in range(2):
                total = jnp.maximum(jnp.sum(totals[i][...], axis=1, keepdims=True), 1e-30)
                lse = peaks[i][:, 0:1] + jnp.log2(total)
                scale = 1.0 / total
                for k in range(tile_heads):
                    h = (r * 2 + i) * tile_heads + k
                    rows = slice(k * tokens, (k + 1) * tokens)
                    mixed = (accs[i][rows, :] * scale[rows, :]).astype(jnp.bfloat16)
                    out = jnp.dot(mixed, wv[h], preferred_element_type=jnp.float32)
                    o_ref[:, pl.ds(pl.multiple_of(h * vd, vd), vd)] = out.astype(jnp.bfloat16)
                    lse_tile = place_log(lse_tile, lane, h, lse[rows, :])
            return lse_tile

        lse_tile = lax.fori_loop(
            0, rows_each // (2 * tile), row_pair, jnp.zeros((tokens, 128), jnp.float32)
        )
        o_ref[:, heads * vd :] = lse_tile.astype(jnp.bfloat16)

    for j in range(n):
        work(j)
    if keep:
        for j in range(n):
            pltpu.make_async_copy(kts[j], kept[j], keep_sems.at[j]).wait()


def place_log(tile, lane, h, value):
    high = value.astype(jnp.bfloat16).astype(jnp.float32)
    middle = (value - high).astype(jnp.bfloat16).astype(jnp.float32)
    low = value - high - middle
    tile = jnp.where(lane == h, high, tile)
    tile = jnp.where(lane == h + 32, middle, tile)
    return jnp.where(lane == h + 64, low, tile)


def attend(metas, queries, jobs, own, sib, w_absorb, w_value, depth, row_tile, saved=None, keep=False):
    fresh = saved is None
    tokens = queries[0].shape[0]
    heads, nope, lat = w_absorb.shape
    vd = w_value.shape[2]
    width = own.shape[0]
    slots = [-(-depth * len(job[0]) // SMALL) * SMALL for job in jobs]
    rows = heads * tokens
    tile = min(row_tile, rows // 2)
    keys = sum(slots) * BT * 2 // 3
    any_space = pl.BlockSpec(memory_space=pl.ANY)
    vmem = pl.BlockSpec(memory_space=pltpu.VMEM)
    smem = pl.BlockSpec(memory_space=pltpu.SMEM)
    lists = sum(slots) + 2 * len(jobs)
    kt_shapes = [(width, s * BT) for s in slots]
    out_shape = [jax.ShapeDtypeStruct((tokens, heads * vd + 128), jnp.bfloat16) for _ in jobs]
    out_specs = [vmem for _ in jobs]
    if keep:
        out_shape += [jax.ShapeDtypeStruct(s, jnp.bfloat16) for s in kt_shapes]
        out_shape += [jax.ShapeDtypeStruct((lists,), jnp.int32)]
        out_specs += [any_space] * len(jobs) + [smem]
    in_specs = [smem] + [vmem] * len(jobs) + [any_space] * 4
    operands = [jnp.concatenate(metas), *queries, w_absorb, own, sib, w_value]
    if not fresh:
        in_specs += [any_space] * len(jobs) + [smem]
        operands += saved
    scratch = []
    if fresh:
        scratch += [pltpu.VMEM((s, width, WIDE), jnp.bfloat16) for s in slots]
    scratch += [pltpu.VMEM(s, jnp.bfloat16) for s in kt_shapes]
    scratch += [
        pltpu.VMEM((len(jobs) * rows, width), jnp.bfloat16),
        pltpu.VMEM(w_absorb.shape, jnp.bfloat16),
        pltpu.VMEM(w_value.shape, jnp.bfloat16),
        *[pltpu.VMEM((tile, lat), jnp.float32)] * 2,
        *[pltpu.VMEM((tile, CHUNK * BT), jnp.float32)] * 2,
        *[pltpu.VMEM((tile, 128), jnp.float32)] * 4,
    ]
    if fresh and not keep:
        scratch += [pltpu.SMEM((lists,), jnp.int32)]
    scratch += [
        pltpu.SMEM((64,), jnp.int32),
        pltpu.SemaphoreType.DMA,
        pltpu.SemaphoreType.DMA,
        pltpu.SemaphoreType.DMA((len(jobs),)),
        pltpu.SemaphoreType.DMA((len(jobs),)),
    ]
    return pl.pallas_call(
        functools.partial(attend_kernel, own.shape[1] // BT, jobs, fresh, keep),
        out_shape=out_shape,
        in_specs=in_specs,
        out_specs=out_specs,
        scratch_shapes=scratch,
        compiler_params=pltpu.CompilerParams(vmem_limit_bytes=56 * MIB),
        cost_estimate=pl.CostEstimate(
            flops=2 * rows * keys * (width + lat),
            bytes_accessed=2 * keys * width * 2,
            transcendentals=rows * keys,
        ),
    )(*operands)


def read_log(ref, rows, heads):
    tail = ref[rows, ref.shape[1] - 128 :].astype(jnp.float32)
    return tail[:, 0:heads] + tail[:, 32 : 32 + heads] + tail[:, 64 : 64 + heads]


def merge(parts, heads, out, out_rows, with_log):
    vd = (parts[0][0].shape[1] - 128) // heads
    logs = [read_log(ref, rows, heads) for ref, rows in parts]
    peak = functools.reduce(jnp.maximum, logs)
    shares = [jnp.exp2(value - peak) for value in logs]
    total = functools.reduce(jnp.add, shares)
    norm = 1.0 / total
    for h in range(heads):
        columns = slice(h * vd, (h + 1) * vd)
        mixed = sum(
            ref[rows, columns].astype(jnp.float32) * (share * norm)[:, h : h + 1]
            for (ref, rows), share in zip(parts, shares)
        )
        out[out_rows, columns] = mixed.astype(jnp.bfloat16)
    if with_log:
        log = peak + jnp.log2(total)
        tokens = log.shape[0]
        lane = lax.broadcasted_iota(jnp.int32, (tokens, 128), 1)
        tile = jnp.zeros((tokens, 128), jnp.float32)
        for h in range(heads):
            tile = place_log(tile, lane, h, log[:, h : h + 1])
        out[out_rows, heads * vd :] = tile.astype(jnp.bfloat16)


def small_call(kernel, shape, operands):
    vmem = pl.BlockSpec(memory_space=pltpu.VMEM)
    return pl.pallas_call(
        kernel,
        out_shape=jax.ShapeDtypeStruct(shape, jnp.bfloat16),
        in_specs=[vmem] * len(operands),
        out_specs=vmem,
        compiler_params=pltpu.CompilerParams(vmem_limit_bytes=16 * MIB),
        cost_estimate=pl.CostEstimate(
            flops=4 * shape[0] * shape[1], bytes_accessed=8 * shape[0] * shape[1], transcendentals=0
        ),
    )(*operands)


def combine(partials, heads):
    tokens = min(p.shape[0] for p, _ in partials)
    columns = partials[0][0].shape[1]

    def kernel(*refs):
        parts = [(ref, slice(r, r + tokens)) for ref, (_, r) in zip(refs, partials)]
        merge(parts, heads, refs[-1], slice(0, tokens), False)

    return small_call(kernel, (tokens, columns - 128), [p for p, _ in partials])


def pack_for_other(far, near, near_row, side, heads):
    tokens, columns = far.shape

    def kernel(far_ref, near_ref, side_ref, out):
        out[0:tokens, :] = far_ref[...]
        parts = [(near_ref, slice(near_row, near_row + tokens)), (side_ref, slice(0, tokens))]
        merge(parts, heads, out, slice(tokens, 2 * tokens), True)

    return small_call(kernel, (2 * tokens, columns), [far, near, side])


def settle(sent, got, heads):
    rows, columns = sent.shape
    half = rows // 2
    low, high = slice(0, half), slice(half, rows)

    def kernel(sent_ref, got_ref, out):
        merge([(sent_ref, high), (got_ref, low)], heads, out, low, False)
        merge([(sent_ref, low), (got_ref, high)], heads, out, high, False)

    return small_call(kernel, (rows, columns - 128), [sent, got])


def project_kernel(x_ref, w_ref, o_ref):
    o_ref[...] = jnp.dot(x_ref[...], w_ref[...], preferred_element_type=jnp.float32).astype(jnp.bfloat16)


def project(x, w):
    rows, depth = x.shape
    columns = w.shape[1]
    wide = 256 if columns % 256 == 0 else columns
    return pl.pallas_call(
        project_kernel,
        out_shape=jax.ShapeDtypeStruct((rows, columns), jnp.bfloat16),
        grid=(columns // wide,),
        in_specs=[
            pl.BlockSpec((rows, depth), lambda j: (0, 0)),
            pl.BlockSpec((depth, wide), lambda j: (0, j)),
        ],
        out_specs=pl.BlockSpec((rows, wide), lambda j: (0, j)),
        compiler_params=pltpu.CompilerParams(vmem_limit_bytes=60 * MIB),
        cost_estimate=pl.CostEstimate(
            flops=2 * rows * depth * columns,
            bytes_accessed=2 * (rows * depth + depth * columns + rows * columns),
            transcendentals=0,
        ),
    )(x, w)


def body(queries, latent, selection, span_offset, w_absorb, w_value, w_out):
    owners = lax.axis_size("ctx")
    groups = lax.axis_size("head")
    me = lax.axis_index("ctx")
    column = lax.axis_index("head")
    chips = owners // 2
    depth = 3 * selection.shape[1] // (2 * owners)
    heads = w_absorb.shape[0]
    tokens = queries.shape[0]
    piece = tokens // PIECES
    sibling = [(i, i ^ 1) for i in range(owners)]
    turns = range(1, chips)
    ahead = {t: [(i, (i + 2 * t) % owners) for i in range(owners)] for t in turns}
    back = {t: [(i, (i - 2 * t) % owners) for i in range(owners)] for t in turns}
    own = latent.T

    def meta_of(row, index):
        return jnp.concatenate(
            [row[0], jnp.stack([span_offset[0] + index * tokens, me, me ^ 1])]
        ).astype(jnp.int32)

    far_queries = {t: lax.ppermute(queries, "ctx", ahead[t]) for t in turns}
    sib = lax.ppermute(own, "ctx", sibling)
    far_rows = {t: lax.ppermute(selection, "ctx", ahead[t]) for t in turns}
    my_meta = meta_of(selection, me)
    metas = [meta_of(far_rows[t], (me - 2 * t) % owners) for t in turns] + [my_meta]
    (near,) = attend(
        [my_meta], [queries], [(("own",), tokens, 0)], own, own, w_absorb, w_value, depth, 1024
    )
    outputs = []
    saved = None
    pieces = []
    last = near
    for c in range(PIECES):
        rows = slice(c * piece, (c + 1) * piece)
        jobs = [(("own", "sib"), tokens, c * piece) for _ in turns] + [(("sib",), tokens, c * piece)]
        cuts = [far_queries[t][rows] for t in turns] + [queries[rows]]
        *cuts, last = lax.optimization_barrier((*cuts, last))
        results = attend(
            metas, cuts, jobs, own, sib, w_absorb, w_value, depth, 512, saved, saved is None
        )
        if saved is None:
            saved = list(results[len(jobs) :])
        fars, side = results[: len(jobs) - 1], results[len(jobs) - 1]
        if chips == 2:
            sent = pack_for_other(fars[0], near, c * piece, side, heads)
            last = sent
            pieces.append((sent, lax.ppermute(sent, "ctx", ahead[1])))
        else:
            arrived = [lax.ppermute(far, "ctx", back[t]) for t, far in zip(turns, fars)]
            pieces.append(combine([(a, 0) for a in arrived] + [(side, 0), (near, c * piece)], heads))
    for c in range(PIECES):
        if chips == 2:
            sent, got = pieces[c]
            mine = settle(sent, got, heads)
        else:
            mine = pieces[c]
            mine = jnp.concatenate([mine] + [lax.ppermute(mine, "ctx", ahead[t]) for t in turns], axis=0)
        pair = jnp.concatenate([mine, lax.ppermute(mine, "ctx", sibling)], axis=0)
        shares = project(pair, w_out)

        def share_of(block):
            turn = (me // 2 - block // 2) % chips
            place = (me + block) % 2 * chips + turn
            return lax.dynamic_slice_in_dim(shares, place * piece, piece, 0)

        arrived = [share_of(column)]
        for s in sorted(range(1, groups), key=lambda s: -min(s, groups - s)):
            shift = [(i, (i + s) % groups) for i in range(groups)]
            arrived.append(lax.ppermute(share_of((column + s) % groups), "head", shift))
        outputs.append(sum(a.astype(jnp.float32) for a in arrived).astype(jnp.bfloat16))
    return jnp.concatenate(outputs, axis=0)


def solution(mesh):
    placed = (
        P(("groups", "ctx"), "head"),
        P(("groups", "ctx"), None),
        P(("groups", "ctx"), None),
        P("groups"),
        P("head", None, None),
        P("head", None, None),
        P("head", "ctx"),
    )
    return jax.shard_map(
        body, mesh=mesh, in_specs=placed, out_specs=P(("groups", "head"), "ctx"), check_vma=False
    )
```

```python
import functools
import math

import jax
import jax.numpy as jnp
from jax import lax
from jax.experimental import pallas as pl
from jax.experimental.pallas import tpu as pltpu
from jax.sharding import PartitionSpec as P

BT = 64
WIDE = 128
CHUNK = 8
SMALL = 4
PIECES = 2
NEVER = -1e30
FAR = 1 << 30
MIB = 1024 * 1024
META = 68


def attend_kernel(blocks_held, jobs, fresh, keep, *refs):
    refs = list(refs)
    n = len(jobs)

    def take(k):
        out = refs[:k]
        del refs[:k]
        return out

    (meta,) = take(1)
    queries = take(n)
    wa_hbm, own_hbm, sib_hbm, wv_hbm = take(4)
    saved = [] if fresh else take(n)
    outs = take(n)
    kept = take(n) if keep else []
    raws = take(n) if fresh else []
    kts = take(n)
    q_full, wa, wv = take(3)
    accs, stores, peaks, totals = take(2), take(2), take(2), take(2)
    wa_sem, wv_sem, kv_sems, keep_sems = take(4)

    tokens = queries[0].shape[0]
    heads, nope, lat = wa.shape
    width = kts[0].shape[0]
    vd = wv.shape[2]
    head_width = nope + width - lat
    fold = head_width ** -0.5 * math.log2(math.e)

    def slots_of(j):
        return (meta[META * j + 65] + SMALL - 1) // SMALL * SMALL

    def gather(j):
        row0 = META * j
        count, mine = meta[row0 + 65], meta[row0 + 67]
        raw, sem = raws[j], kv_sems.at[j]

        def fetch(i, _):
            block = meta[row0 + i]
            col = pl.multiple_of((block % blocks_held) // 2 * WIDE, WIDE)
            here = (block // blocks_held == mine) | (i >= count)

            @pl.when(here)
            def _():
                pltpu.make_async_copy(own_hbm.at[:, pl.ds(col, WIDE)], raw.at[i], sem).start()

            @pl.when(jnp.logical_not(here))
            def _():
                pltpu.make_async_copy(sib_hbm.at[:, pl.ds(col, WIDE)], raw.at[i], sem).start()

            return 0

        lax.fori_loop(0, slots_of(j), fetch, 0)

    def join(j):
        raw, kt, row0 = raws[j], kts[j], META * j
        slots = slots_of(j)

        def land(i, _):
            pltpu.make_async_copy(own_hbm.at[:, pl.ds(0, WIDE)], raw.at[0], kv_sems.at[j]).wait()
            return 0

        lax.fori_loop(0, slots, land, 0)

        def pair(i, _):
            left = raw[2 * i]
            right = raw[2 * i + 1]
            left_swapped = jnp.concatenate([left[:, BT:], left[:, :BT]], axis=1)
            right_swapped = jnp.concatenate([right[:, BT:], right[:, :BT]], axis=1)
            low = jnp.where(meta[row0 + 2 * i] % 2 == 1, left_swapped, left)
            high = jnp.where(meta[row0 + 2 * i + 1] % 2 == 1, right, right_swapped)
            lane = lax.broadcasted_iota(jnp.int32, (width, WIDE), 1)
            kt[:, pl.ds(pl.multiple_of(i * WIDE, WIDE), WIDE)] = jnp.where(lane < BT, low, high)
            return 0

        lax.fori_loop(0, slots // 2, pair, 0)

    rows_each = heads * tokens

    def absorb(j):
        for h in range(heads):
            base = h * head_width
            latent_part = jnp.dot(
                queries[j][:, base : base + nope], wa[h], preferred_element_type=jnp.float32
            )
            rows = slice(j * rows_each + h * tokens, j * rows_each + (h + 1) * tokens)
            q_full[rows, 0:lat] = (latent_part * fold).astype(jnp.bfloat16)
            turned = queries[j][:, base + nope : base + head_width].astype(jnp.float32)
            q_full[rows, lat:width] = (turned * fold).astype(jnp.bfloat16)

    def held(j):
        return kts[j].at[:, 0 : kts[j].shape[1] - CHUNK * BT]

    wa_copy = pltpu.make_async_copy(wa_hbm, wa, wa_sem)
    wv_copy = pltpu.make_async_copy(wv_hbm, wv, wv_sem)
    wa_copy.start()
    for j in range(n):
        if fresh:
            gather(j)
        else:
            pltpu.make_async_copy(saved[j], held(j), kv_sems.at[j]).start()
        if j == 0:
            wv_copy.start()
    wa_copy.wait()

    tile = accs[0].shape[0]
    tile_heads = tile // tokens
    lane = lax.broadcasted_iota(jnp.int32, (tokens, 128), 1)

    def work(j):
        kt, list0, o_ref = kts[j], META * j, outs[j]
        first = meta[list0 + 66] + jobs[j][1]
        full = meta[list0 + 64]
        count = meta[list0 + 65]
        plain_chunks = full // CHUNK
        done = plain_chunks * CHUNK
        small_chunks = (count - done + SMALL - 1) // SMALL

        def row_pair(r, lse_tile):
            row0 = j * rows_each + r * 2 * tile
            bases = [pl.multiple_of(row0, tile), pl.multiple_of(row0 + tile, tile)]
            for i in range(2):
                accs[i][...] = jnp.zeros_like(accs[i])
                peaks[i][...] = jnp.full(peaks[i].shape, NEVER, jnp.float32)
                totals[i][...] = jnp.zeros_like(totals[i])

            def score(i, key0, n):
                stores[i][:, 0 : n * BT] = jnp.dot(
                    q_full[pl.ds(bases[i], tile), :], kt[:, pl.ds(key0, n * BT)],
                    preferred_element_type=jnp.float32,
                )

            def soften(i, n, visible):
                scores = stores[i][:, 0 : n * BT]
                if visible is not None:
                    scores = jnp.where(
                        visible[None], scores.reshape(tile_heads, tokens, n * BT), NEVER
                    ).reshape(tile, n * BT)
                peak = peaks[i][...]
                new_peak = jnp.maximum(peak, jnp.max(scores, axis=1, keepdims=True))
                peaks[i][...] = new_peak
                raised = jnp.exp2(scores - new_peak[:, 0:1])
                keep_share = jnp.exp2(peak - new_peak)
                total = totals[i][...] * keep_share
                for k in range(n * BT // 128):
                    total = total + raised[:, k * 128 : (k + 1) * 128]
                totals[i][...] = total
                return raised.astype(jnp.bfloat16), keep_share[:, 0:1]

            def mix(i, key0, n, raised, keep_share):
                accs[i][...] = accs[i][...] * keep_share + lax.dot_general(
                    raised, kt[0:lat, pl.ds(key0, n * BT)], (((1,), (1,)), ((), ())),
                    preferred_element_type=jnp.float32,
                )

            def chunk(n, start, masked, c, _):
                key0 = pl.multiple_of(start + c * n * BT, 128)
                key1 = pl.multiple_of(key0 + n * BT, 128)
                visible = None
                if masked:
                    block0 = key0 // BT
                    column = lax.broadcasted_iota(jnp.int32, (tokens, n * BT), 1)
                    position = jnp.zeros((tokens, n * BT), jnp.int32)
                    for b in range(n):
                        at = jnp.where(
                            block0 + b < full, 0,
                            jnp.where(block0 + b < count, meta[list0 + block0 + b] * BT, FAR),
                        )
                        position = jnp.where(column // BT == b, at + column % BT, position)
                    query = first + lax.broadcasted_iota(jnp.int32, (tokens, n * BT), 0)
                    visible = position <= query
                score(1, key0, n)
                raised, share = soften(0, n, visible)
                mix(0, key0, n, raised, share)
                score(0, key1, n)
                raised, share = soften(1, n, visible)
                mix(1, key0, n, raised, share)
                return 0

            @pl.when(plain_chunks > 0)
            def _():
                score(0, 0, CHUNK)

            @pl.when(plain_chunks == 0)
            def _():
                score(0, 0, SMALL)

            lax.fori_loop(0, plain_chunks, functools.partial(chunk, CHUNK, 0, False), 0)
            lax.fori_loop(0, small_chunks, functools.partial(chunk, SMALL, done * BT, True), 0)

            for i in range(2):
                total = jnp.maximum(jnp.sum(totals[i][...], axis=1, keepdims=True), 1e-30)
                lse = peaks[i][:, 0:1] + jnp.log2(total)
                scale = 1.0 / total
                for k in range(tile_heads):
                    h = (r * 2 + i) * tile_heads + k
                    rows = slice(k * tokens, (k + 1) * tokens)
                    mixed = (accs[i][rows, :] * scale[rows, :]).astype(jnp.bfloat16)
                    out = jnp.dot(mixed, wv[h], preferred_element_type=jnp.float32)
                    o_ref[:, pl.ds(pl.multiple_of(h * vd, vd), vd)] = out.astype(jnp.bfloat16)
                    lse_tile = place_log(lse_tile, lane, h, lse[rows, :])
            return lse_tile

        lse_tile = lax.fori_loop(
            0, rows_each // (2 * tile), row_pair, jnp.zeros((tokens, 128), jnp.float32)
        )
        o_ref[:, heads * vd :] = lse_tile.astype(jnp.bfloat16)

    for j in range(n):
        absorb(j)
        if fresh:
            join(j)
        else:
            pltpu.make_async_copy(saved[j], held(j), kv_sems.at[j]).wait()
        if keep:
            pltpu.make_async_copy(held(j), kept[j], keep_sems.at[j]).start()
        if j == 0:
            wv_copy.wait()
        work(j)
    if keep:
        for j in range(n):
            pltpu.make_async_copy(held(j), kept[j], keep_sems.at[j]).wait()


def place_log(tile, lane, h, value):
    high = value.astype(jnp.bfloat16).astype(jnp.float32)
    middle = (value - high).astype(jnp.bfloat16).astype(jnp.float32)
    low = value - high - middle
    tile = jnp.where(lane == h, high, tile)
    tile = jnp.where(lane == h + 32, middle, tile)
    return jnp.where(lane == h + 64, low, tile)


def attend(metas, queries, jobs, own, sib, w_absorb, w_value, depth, row_tile, saved=None, keep=False):
    fresh = saved is None
    tokens = queries[0].shape[0]
    heads, nope, lat = w_absorb.shape
    vd = w_value.shape[2]
    width = own.shape[0]
    slots = [-(-depth * job[0] // SMALL) * SMALL for job in jobs]
    rows = heads * tokens
    tile = min(row_tile, rows // 2)
    keys = sum(slots) * BT * 2 // 3
    any_space = pl.BlockSpec(memory_space=pl.ANY)
    vmem = pl.BlockSpec(memory_space=pltpu.VMEM)
    smem = pl.BlockSpec(memory_space=pltpu.SMEM)
    out_shape = [jax.ShapeDtypeStruct((tokens, heads * vd + 128), jnp.bfloat16) for _ in jobs]
    out_specs = [vmem for _ in jobs]
    if keep:
        out_shape += [jax.ShapeDtypeStruct((width, s * BT), jnp.bfloat16) for s in slots]
        out_specs += [any_space] * len(jobs)
    in_specs = [smem] + [vmem] * len(jobs) + [any_space] * 4
    operands = [metas, *queries, w_absorb, own, sib, w_value]
    if not fresh:
        in_specs += [any_space] * len(jobs)
        operands += saved
    scratch = []
    if fresh:
        scratch += [pltpu.VMEM((s, width, WIDE), jnp.bfloat16) for s in slots]
    scratch += [pltpu.VMEM((width, (s + CHUNK) * BT), jnp.bfloat16) for s in slots]
    scratch += [
        pltpu.VMEM((len(jobs) * rows, width), jnp.bfloat16),
        pltpu.VMEM(w_absorb.shape, jnp.bfloat16),
        pltpu.VMEM(w_value.shape, jnp.bfloat16),
        *[pltpu.VMEM((tile, lat), jnp.float32)] * 2,
        *[pltpu.VMEM((tile, CHUNK * BT), jnp.float32)] * 2,
        *[pltpu.VMEM((tile, 128), jnp.float32)] * 4,
        pltpu.SemaphoreType.DMA,
        pltpu.SemaphoreType.DMA,
        pltpu.SemaphoreType.DMA((len(jobs),)),
        pltpu.SemaphoreType.DMA((len(jobs),)),
    ]
    return pl.pallas_call(
        functools.partial(attend_kernel, own.shape[1] // BT, jobs, fresh, keep),
        out_shape=out_shape,
        in_specs=in_specs,
        out_specs=out_specs,
        scratch_shapes=scratch,
        compiler_params=pltpu.CompilerParams(vmem_limit_bytes=44 * MIB),
        cost_estimate=pl.CostEstimate(
            flops=2 * rows * keys * (width + lat),
            bytes_accessed=2 * keys * width * 2,
            transcendentals=rows * keys,
        ),
    )(*operands)


def read_log(ref, rows, heads):
    tail = ref[rows, ref.shape[1] - 128 :].astype(jnp.float32)
    return tail[:, 0:heads] + tail[:, 32 : 32 + heads] + tail[:, 64 : 64 + heads]


def merge(parts, heads, out, out_rows, with_log):
    vd = (parts[0][0].shape[1] - 128) // heads
    logs = [read_log(ref, rows, heads) for ref, rows in parts]
    peak = functools.reduce(jnp.maximum, logs)
    shares = [jnp.exp2(value - peak) for value in logs]
    total = functools.reduce(jnp.add, shares)
    norm = 1.0 / total
    for h in range(heads):
        columns = slice(h * vd, (h + 1) * vd)
        mixed = sum(
            ref[rows, columns].astype(jnp.float32) * (share * norm)[:, h : h + 1]
            for (ref, rows), share in zip(parts, shares)
        )
        out[out_rows, columns] = mixed.astype(jnp.bfloat16)
    if with_log:
        log = peak + jnp.log2(total)
        tokens = log.shape[0]
        lane = lax.broadcasted_iota(jnp.int32, (tokens, 128), 1)
        tile = jnp.zeros((tokens, 128), jnp.float32)
        for h in range(heads):
            tile = place_log(tile, lane, h, log[:, h : h + 1])
        out[out_rows, heads * vd :] = tile.astype(jnp.bfloat16)


def small_call(kernel, shape, operands):
    vmem = pl.BlockSpec(memory_space=pltpu.VMEM)
    return pl.pallas_call(
        kernel,
        out_shape=jax.ShapeDtypeStruct(shape, jnp.bfloat16),
        in_specs=[vmem] * len(operands),
        out_specs=vmem,
        compiler_params=pltpu.CompilerParams(vmem_limit_bytes=16 * MIB),
        cost_estimate=pl.CostEstimate(flops=1, bytes_accessed=1, transcendentals=0),
    )(*operands)


def combine(partials, heads):
    tokens = min(p.shape[0] for p, _ in partials)
    columns = partials[0][0].shape[1]

    def kernel(*refs):
        parts = [(ref, slice(r, r + tokens)) for ref, (_, r) in zip(refs, partials)]
        merge(parts, heads, refs[-1], slice(0, tokens), False)

    return small_call(kernel, (tokens, columns - 128), [p for p, _ in partials])


def pack_for_other(far, near, near_row, side, heads):
    tokens, columns = far.shape

    def kernel(far_ref, near_ref, side_ref, out):
        out[0:tokens, :] = far_ref[...]
        parts = [(near_ref, slice(near_row, near_row + tokens)), (side_ref, slice(0, tokens))]
        merge(parts, heads, out, slice(tokens, 2 * tokens), True)

    return small_call(kernel, (2 * tokens, columns), [far, near, side])


def settle(sent, got, heads):
    rows, columns = sent.shape
    half = rows // 2
    low, high = slice(0, half), slice(half, rows)

    def kernel(sent_ref, got_ref, out):
        merge([(sent_ref, high), (got_ref, low)], heads, out, low, False)
        merge([(sent_ref, low), (got_ref, high)], heads, out, high, False)

    return small_call(kernel, (rows, columns - 128), [sent, got])


def project_kernel(x_ref, w_ref, o_ref):
    o_ref[...] = jnp.dot(x_ref[...], w_ref[...], preferred_element_type=jnp.float32).astype(jnp.bfloat16)


def project(x, w):
    rows, depth = x.shape
    columns = w.shape[1]
    wide = 256 if columns % 256 == 0 else columns
    return pl.pallas_call(
        project_kernel,
        out_shape=jax.ShapeDtypeStruct((rows, columns), jnp.bfloat16),
        grid=(columns // wide,),
        in_specs=[
            pl.BlockSpec((rows, depth), lambda j: (0, 0)),
            pl.BlockSpec((depth, wide), lambda j: (0, j)),
        ],
        out_specs=pl.BlockSpec((rows, wide), lambda j: (0, j)),
        compiler_params=pltpu.CompilerParams(vmem_limit_bytes=24 * MIB),
        cost_estimate=pl.CostEstimate(flops=1, bytes_accessed=1, transcendentals=0),
    )(x, w)


def body(queries, latent, selection, span_offset, w_absorb, w_value, w_out):
    owners = lax.axis_size("ctx")
    groups = lax.axis_size("head")
    me = lax.axis_index("ctx")
    column = lax.axis_index("head")
    chips = owners // 2
    depth = 3 * selection.shape[1] // (2 * owners)
    heads = w_absorb.shape[0]
    tokens = queries.shape[0]
    piece = tokens // PIECES
    sibling = [(i, i ^ 1) for i in range(owners)]
    turns = range(1, chips)
    ahead = {t: [(i, (i + 2 * t) % owners) for i in range(owners)] for t in turns}
    back = {t: [(i, (i - 2 * t) % owners) for i in range(owners)] for t in turns}
    own = latent.T

    held = latent.shape[0] // BT

    def lists_of(rows, indices, own_too, sib_too):
        starts = span_offset[0] + indices * tokens
        owner = rows // held
        here = ((owner == (me ^ 1)) & sib_too) | ((owner == me) & own_too)
        full = here & (rows * BT + BT - 1 <= starts[:, None])
        edge = here & ~full & (rows * BT <= starts[:, None] + tokens - 1)
        order = jnp.arange(rows.shape[1])
        before = order[None, :] < order[:, None]
        rank = lambda marks: jnp.sum(marks[:, None, :] & before[None], axis=2, dtype=jnp.int32)
        n_full = jnp.sum(full, axis=1, dtype=jnp.int32)
        n_all = n_full + jnp.sum(edge, axis=1, dtype=jnp.int32)
        slot = jnp.where(full, rank(full), jnp.where(edge, n_full[:, None] + rank(edge), -1))
        listed = jnp.sum(
            jnp.where(slot[:, None, :] == order[None, :, None], rows[:, None, :], 0), axis=2, dtype=jnp.int32
        )
        mine = jnp.full_like(n_all, me)
        tail = jnp.stack([n_full, n_all, starts.astype(jnp.int32), mine], axis=1)
        return jnp.concatenate([listed, tail], axis=1).reshape(-1)

    far_queries = {t: lax.ppermute(queries, "ctx", ahead[t]) for t in turns}
    sib = lax.ppermute(own, "ctx", sibling)
    far_rows = {t: lax.ppermute(selection, "ctx", ahead[t]) for t in turns}
    near_meta = lists_of(selection, me[None], True, False)
    (near,) = attend(near_meta, [queries], [(1, 0)], own, own, w_absorb, w_value, depth, 1024)
    meta = lists_of(
        jnp.concatenate([far_rows[t] for t in turns] + [selection], axis=0),
        jnp.stack([(me - 2 * t) % owners for t in turns] + [me]),
        jnp.arange(chips)[:, None] < chips - 1,
        True,
    )
    outputs = []
    saved = None
    pieces = []
    last = near
    for c in range(PIECES):
        rows = slice(c * piece, (c + 1) * piece)
        jobs = [(2, c * piece)] * (chips - 1) + [(1, c * piece)]
        cuts = [far_queries[t][rows] for t in turns] + [queries[rows]]
        *cuts, last = lax.optimization_barrier((*cuts, last))
        results = attend(
            meta, cuts, jobs, own, sib, w_absorb, w_value, depth, 512, saved, saved is None
        )
        if saved is None:
            saved = list(results[len(jobs) :])
        fars, side = results[: len(jobs) - 1], results[len(jobs) - 1]
        if chips == 2:
            sent = pack_for_other(fars[0], near, c * piece, side, heads)
            last = sent
            pieces.append((sent, lax.ppermute(sent, "ctx", ahead[1])))
        else:
            arrived = [lax.ppermute(far, "ctx", back[t]) for t, far in zip(turns, fars)]
            pieces.append(combine([(a, 0) for a in arrived] + [(side, 0), (near, c * piece)], heads))
    last = [last]
    for c in range(PIECES):
        if chips == 2:
            sent, got = pieces[c]
            got, *last = lax.optimization_barrier((got, *last))
            mine = settle(sent, got, heads)
        else:
            mine = pieces[c]
            mine = jnp.concatenate([mine] + [lax.ppermute(mine, "ctx", ahead[t]) for t in turns], axis=0)
        pair = jnp.concatenate([mine, lax.ppermute(mine, "ctx", sibling)], axis=0)
        shares = project(pair, w_out)

        def share_of(block):
            turn = (me // 2 - block // 2) % chips
            place = (me + block) % 2 * chips + turn
            return lax.dynamic_slice_in_dim(shares, place * piece, piece, 0)

        steps = sorted(range(1, groups), key=lambda s: -min(s, groups - s))
        last = [share_of((column + s) % groups) for s in steps]
        arrived = [share_of(column)] + [
            lax.ppermute(share, "head", [(i, (i + s) % groups) for i in range(groups)])
            for s, share in zip(steps, last)
        ]
        outputs.append(sum(a.astype(jnp.float32) for a in arrived).astype(jnp.bfloat16))
    return jnp.concatenate(outputs, axis=0)


def solution(mesh):
    placed = (
        P(("groups", "ctx"), "head"),
        P(("groups", "ctx"), None),
        P(("groups", "ctx"), None),
        P("groups"),
        P("head", None, None),
        P("head", None, None),
        P("head", "ctx"),
    )
    return jax.shard_map(
        body, mesh=mesh, in_specs=placed, out_specs=P(("groups", "head"), "ctx"), check_vma=False
    )
```

```python
import functools
import math

import jax
import jax.numpy as jnp
from jax import lax
from jax.experimental import pallas as pl
from jax.experimental.pallas import tpu as pltpu
from jax.sharding import PartitionSpec as P

BT = 64
WIDE = 128
CHUNK = 8
SMALL = 4
FIRST = 64
NEVER = -1e30
FAR = 1 << 30
MIB = 1024 * 1024
META = 128


def attend_kernel(
    blocks_held, cuts,
    meta, query_hbm, wa_hbm, own_hbm, sib_hbm, wv_hbm, *refs,
):
    outs, refs = refs[: len(cuts)], refs[len(cuts) :]
    raw, queries, kt, q_full, wa, wv, *refs = refs
    accs, stores, peaks, totals = refs[0:2], refs[2:4], refs[4:6], refs[6:8]
    wa_sem, wv_sem, q_sem, kv_sem = refs[8:]

    tokens = queries.shape[0]
    heads, nope, lat = wa.shape
    width = kt.shape[0]
    vd = wv.shape[2]
    head_width = nope + width - lat
    fold = head_width ** -0.5 * math.log2(math.e)
    full, count, first, mine = meta[64], meta[65], meta[66], meta[67]
    plain_chunks = full // CHUNK
    done = plain_chunks * CHUNK
    small_chunks = (count - done + SMALL - 1) // SMALL
    slots = done + small_chunks * SMALL

    q_copy = pltpu.make_async_copy(query_hbm, queries, q_sem)
    wa_copy = pltpu.make_async_copy(wa_hbm, wa, wa_sem)
    wv_copy = pltpu.make_async_copy(wv_hbm, wv, wv_sem)
    q_copy.start()
    wa_copy.start()

    def fetch(i, _):
        block = meta[i]
        col = pl.multiple_of((block % blocks_held) // 2 * WIDE, WIDE)
        here = (block // blocks_held == mine) | (i >= count)

        @pl.when(here)
        def _():
            pltpu.make_async_copy(own_hbm.at[:, pl.ds(col, WIDE)], raw.at[i], kv_sem).start()

        @pl.when(jnp.logical_not(here))
        def _():
            pltpu.make_async_copy(sib_hbm.at[:, pl.ds(col, WIDE)], raw.at[i], kv_sem).start()

        return 0

    lax.fori_loop(0, slots, fetch, 0)
    wv_copy.start()
    q_copy.wait()
    wa_copy.wait()
    for h in range(heads):
        base = h * head_width
        latent_part = jnp.dot(
            queries[:, base : base + nope], wa[h], preferred_element_type=jnp.float32
        )
        rows = slice(h * tokens, (h + 1) * tokens)
        q_full[rows, 0:lat] = (latent_part * fold).astype(jnp.bfloat16)
        turned = queries[:, base + nope : base + head_width].astype(jnp.float32)
        q_full[rows, lat:width] = (turned * fold).astype(jnp.bfloat16)

    def land(i, _):
        pltpu.make_async_copy(own_hbm.at[:, pl.ds(0, WIDE)], raw.at[0], kv_sem).wait()
        return 0

    lax.fori_loop(0, slots, land, 0)

    def pair(i, _):
        left_odd = meta[2 * i] % 2 == 1
        right_odd = meta[2 * i + 1] % 2 == 1
        target = pl.ds(pl.multiple_of(i * WIDE, WIDE), WIDE)
        lane = lax.broadcasted_iota(jnp.int32, (width, WIDE), 1)

        def swap(x):
            return jnp.concatenate([x[:, BT:], x[:, :BT]], axis=1)

        @pl.when(jnp.logical_not(left_odd) & right_odd)
        def _():
            kt[:, target] = jnp.where(lane < BT, raw[2 * i], raw[2 * i + 1])

        @pl.when(left_odd & right_odd)
        def _():
            kt[:, target] = jnp.where(lane < BT, swap(raw[2 * i]), raw[2 * i + 1])

        @pl.when(jnp.logical_not(left_odd | right_odd))
        def _():
            kt[:, target] = jnp.where(lane < BT, raw[2 * i], swap(raw[2 * i + 1]))

        @pl.when(left_odd & jnp.logical_not(right_odd))
        def _():
            kt[:, target] = swap(jnp.where(lane < BT, raw[2 * i + 1], raw[2 * i]))

        return 0

    lax.fori_loop(0, slots // 2, pair, 0)
    wv_copy.wait()

    tile = accs[0].shape[0]
    tile_heads = tile // tokens
    lane = lax.broadcasted_iota(jnp.int32, (tokens, 128), 1)

    def row_pair(r, lse_tile):
        row0 = r * 2 * tile
        bases = [pl.multiple_of(row0, tile), pl.multiple_of(row0 + tile, tile)]
        for i in range(2):
            accs[i][...] = jnp.zeros_like(accs[i])
            peaks[i][...] = jnp.full(peaks[i].shape, NEVER, jnp.float32)
            totals[i][...] = jnp.zeros_like(totals[i])

        def score(i, key0, n):
            stores[i][:, 0 : n * BT] = jnp.dot(
                q_full[pl.ds(bases[i], tile), :], kt[:, pl.ds(key0, n * BT)],
                preferred_element_type=jnp.float32,
            )

        def soften(i, n, visible):
            scores = stores[i][:, 0 : n * BT]
            if visible is not None:
                scores = jnp.where(
                    visible[None], scores.reshape(tile_heads, tokens, n * BT), NEVER
                ).reshape(tile, n * BT)
            peak = peaks[i][...]
            new_peak = jnp.maximum(peak, jnp.max(scores, axis=1, keepdims=True))
            peaks[i][...] = new_peak
            raised = jnp.exp2(scores - new_peak[:, 0:1])
            keep_share = jnp.exp2(peak - new_peak)
            total = totals[i][...] * keep_share
            for k in range(n * BT // 128):
                total = total + raised[:, k * 128 : (k + 1) * 128]
            totals[i][...] = total
            return raised.astype(jnp.bfloat16), keep_share[:, 0:1]

        def mix(i, key0, n, raised, keep_share):
            accs[i][...] = accs[i][...] * keep_share + lax.dot_general(
                raised, kt[0:lat, pl.ds(key0, n * BT)], (((1,), (1,)), ((), ())),
                preferred_element_type=jnp.float32,
            )

        def chunk(n, start, masked, c, _):
            key0 = pl.multiple_of(start + c * n * BT, 128)
            key1 = pl.multiple_of(key0 + n * BT, 128)
            visible = None
            if masked:
                block0 = key0 // BT
                column = lax.broadcasted_iota(jnp.int32, (tokens, n * BT), 1)
                position = jnp.zeros((tokens, n * BT), jnp.int32)
                for b in range(n):
                    at = jnp.where(
                        block0 + b < full, 0,
                        jnp.where(block0 + b < count, meta[block0 + b] * BT, FAR),
                    )
                    position = jnp.where(column // BT == b, at + column % BT, position)
                query = first + lax.broadcasted_iota(jnp.int32, (tokens, n * BT), 0)
                visible = position <= query
            score(1, key0, n)
            raised, share = soften(0, n, visible)
            mix(0, key0, n, raised, share)
            score(0, key1, n)
            raised, share = soften(1, n, visible)
            mix(1, key0, n, raised, share)
            return 0

        @pl.when(plain_chunks > 0)
        def _():
            score(0, 0, CHUNK)

        @pl.when(plain_chunks == 0)
        def _():
            score(0, 0, SMALL)

        lax.fori_loop(0, plain_chunks, functools.partial(chunk, CHUNK, 0, False), 0)
        lax.fori_loop(0, small_chunks, functools.partial(chunk, SMALL, done * BT, True), 0)

        for i in range(2):
            total = jnp.maximum(jnp.sum(totals[i][...], axis=1, keepdims=True), 1e-30)
            lse = peaks[i][:, 0:1] + jnp.log2(total)
            scale = 1.0 / total
            for k in range(tile_heads):
                h = (r * 2 + i) * tile_heads + k
                rows = slice(k * tokens, (k + 1) * tokens)
                mixed = (accs[i][rows, :] * scale[rows, :]).astype(jnp.bfloat16)
                out = jnp.dot(mixed, wv[h], preferred_element_type=jnp.float32)
                out = out.astype(jnp.bfloat16)
                for ref, (low, high) in zip(outs, cuts):
                    ref[:, pl.ds(pl.multiple_of(h * vd, vd), vd)] = out[low:high, :]
                lse_tile = place_log(lse_tile, lane, h, lse[rows, :])
        return lse_tile

    lse_tile = lax.fori_loop(
        0, heads * tokens // (2 * tile), row_pair, jnp.zeros((tokens, 128), jnp.float32)
    ).astype(jnp.bfloat16)
    for ref, (low, high) in zip(outs, cuts):
        ref[:, heads * vd :] = lse_tile[low:high, :]


def place_log(tile, lane, h, value):
    high = value.astype(jnp.bfloat16).astype(jnp.float32)
    middle = (value - high).astype(jnp.bfloat16).astype(jnp.float32)
    low = value - high - middle
    tile = jnp.where(lane == h, high, tile)
    tile = jnp.where(lane == h + 32, middle, tile)
    return jnp.where(lane == h + 64, low, tile)


def attend(meta, queries, own, sib, w_absorb, w_value, slots, row_tile, cuts):
    tokens = queries.shape[0]
    heads, nope, lat = w_absorb.shape
    vd = w_value.shape[2]
    width = own.shape[0]
    slots = -(-slots // SMALL) * SMALL
    rows = heads * tokens
    tile = min(row_tile, rows // 2)
    keys = slots * BT * 2 // 3
    any_space = pl.BlockSpec(memory_space=pl.ANY)
    vmem = pl.BlockSpec(memory_space=pltpu.VMEM)
    smem = pl.BlockSpec(memory_space=pltpu.SMEM)
    return pl.pallas_call(
        functools.partial(attend_kernel, own.shape[1] // BT, cuts),
        out_shape=[
            jax.ShapeDtypeStruct((high - low, heads * vd + 128), jnp.bfloat16) for low, high in cuts
        ],
        in_specs=[smem] + [any_space] * 5,
        out_specs=[vmem] * len(cuts),
        scratch_shapes=[
            pltpu.VMEM((slots, width, WIDE), jnp.bfloat16),
            pltpu.VMEM(queries.shape, jnp.bfloat16),
            pltpu.VMEM((width, (slots + CHUNK) * BT), jnp.bfloat16),
            pltpu.VMEM((rows, width), jnp.bfloat16),
            pltpu.VMEM(w_absorb.shape, jnp.bfloat16),
            pltpu.VMEM(w_value.shape, jnp.bfloat16),
            *[pltpu.VMEM((tile, lat), jnp.float32)] * 2,
            *[pltpu.VMEM((tile, CHUNK * BT), jnp.float32)] * 2,
            *[pltpu.VMEM((tile, 128), jnp.float32)] * 4,
            *[pltpu.SemaphoreType.DMA] * 4,
        ],
        compiler_params=pltpu.CompilerParams(vmem_limit_bytes=50 * MIB),
        cost_estimate=pl.CostEstimate(
            flops=2 * rows * keys * (width + lat),
            bytes_accessed=2 * keys * width * 2,
            transcendentals=rows * keys,
        ),
    )(meta.reshape(-1), queries, w_absorb, own, sib, w_value)


def read_log(ref, rows, heads):
    tail = ref[rows, ref.shape[1] - 128 :].astype(jnp.float32)
    return tail[:, 0:heads] + tail[:, 32 : 32 + heads] + tail[:, 64 : 64 + heads]


def merge(parts, heads, out, out_rows, with_log):
    vd = (parts[0][0].shape[1] - 128) // heads
    logs = [read_log(ref, rows, heads) for ref, rows in parts]
    peak = functools.reduce(jnp.maximum, logs)
    shares = [jnp.exp2(value - peak) for value in logs]
    total = functools.reduce(jnp.add, shares)
    norm = 1.0 / total
    for h in range(heads):
        columns = slice(h * vd, (h + 1) * vd)
        mixed = sum(
            ref[rows, columns].astype(jnp.float32) * (share * norm)[:, h : h + 1]
            for (ref, rows), share in zip(parts, shares)
        )
        out[out_rows, columns] = mixed.astype(jnp.bfloat16)
    if with_log:
        log = peak + jnp.log2(total)
        tokens = log.shape[0]
        lane = lax.broadcasted_iota(jnp.int32, (tokens, 128), 1)
        tile = jnp.zeros((tokens, 128), jnp.float32)
        for h in range(heads):
            tile = place_log(tile, lane, h, log[:, h : h + 1])
        out[out_rows, heads * vd :] = tile.astype(jnp.bfloat16)


def small_call(kernel, shape, operands):
    vmem = pl.BlockSpec(memory_space=pltpu.VMEM)
    return pl.pallas_call(
        kernel,
        out_shape=jax.ShapeDtypeStruct(shape, jnp.bfloat16),
        in_specs=[vmem] * len(operands),
        out_specs=vmem,
        compiler_params=pltpu.CompilerParams(vmem_limit_bytes=16 * MIB),
        cost_estimate=pl.CostEstimate(flops=1, bytes_accessed=1, transcendentals=0),
    )(*operands)


def combine(partials, heads, with_log):
    tokens, columns = partials[0].shape

    def kernel(*refs):
        rows = slice(0, tokens)
        merge([(ref, rows) for ref in refs[:-1]], heads, refs[-1], rows, with_log)

    return small_call(kernel, (tokens, columns if with_log else columns - 128), partials)


def settle(near, far_near, far, got, low, heads):
    rows, columns = far.shape
    cut, whole = slice(low, low + rows), slice(0, rows)

    def kernel(near_ref, far_near_ref, far_ref, got_ref, out):
        merge([(near_ref, cut), (got_ref, whole)], heads, out, whole, False)
        merge([(far_near_ref, cut), (far_ref, whole)], heads, out, slice(rows, 2 * rows), False)

    return small_call(kernel, (2 * rows, columns - 128), [near, far_near, far, got])


def project_kernel(steps, mine_ref, other_ref, w_hbm, o_ref, w, acc, sems):
    depth = w.shape[0] // steps
    copies = [
        pltpu.make_async_copy(w_hbm.at[k * depth : (k + 1) * depth, :], w.at[k * depth : (k + 1) * depth, :], sems.at[k])
        for k in range(steps)
    ]
    for copy in copies:
        copy.start()
    for k, copy in enumerate(copies):
        rows = slice(k * depth, (k + 1) * depth)
        x = jnp.concatenate([mine_ref[:, rows], other_ref[:, rows]], axis=0)
        copy.wait()
        part = jnp.dot(x, w[rows, :], preferred_element_type=jnp.float32)
        if k > 0:
            part = acc[...] + part
        if k < steps - 1:
            acc[...] = part
        else:
            o_ref[...] = part.astype(jnp.bfloat16)


def project(mine, other, w):
    rows, depth = mine.shape
    columns = w.shape[1]
    steps = 4
    vmem = pl.BlockSpec(memory_space=pltpu.VMEM)
    return pl.pallas_call(
        functools.partial(project_kernel, steps),
        out_shape=jax.ShapeDtypeStruct((2 * rows, columns), jnp.bfloat16),
        in_specs=[vmem, vmem, pl.BlockSpec(memory_space=pltpu.HBM)],
        out_specs=vmem,
        scratch_shapes=[
            pltpu.VMEM(w.shape, jnp.bfloat16),
            pltpu.VMEM((2 * rows, columns), jnp.float32),
            pltpu.SemaphoreType.DMA((steps,)),
        ],
        compiler_params=pltpu.CompilerParams(vmem_limit_bytes=50 * MIB),
        cost_estimate=pl.CostEstimate(flops=1, bytes_accessed=1, transcendentals=0),
    )(mine, other, w)


def list_kernel(owners, held, tokens, turns, flags, me_ref, offset_ref, *refs):
    outs = refs[-len(turns) :]
    refs = refs[: -len(turns)]
    me = me_ref[0]
    count = refs[0].shape[1]
    row = lax.broadcasted_iota(jnp.int32, (count, count), 0)
    col = lax.broadcasted_iota(jnp.int32, (count, count), 1)
    before = (row < col).astype(jnp.float32)
    lane = lax.broadcasted_iota(jnp.int32, (1, META), 1)
    for j, turn in enumerate(turns):
        blocks = refs[min(j, len(refs) - 1)][...]
        start = offset_ref[0] + lax.rem(me - 2 * turn + owners, owners) * tokens
        here = jnp.zeros(blocks.shape, jnp.bool_)
        for wanted, holder in zip(flags[j], (me, me ^ 1)):
            if wanted:
                here = here | ((blocks >= holder * held) & (blocks < (holder + 1) * held))
        seen = blocks * BT + (BT - 1) <= start
        full = jnp.where(here & seen, 1.0, 0.0)
        edge = jnp.where(
            here & jnp.logical_not(seen) & (blocks * BT <= start + tokens - 1), 1.0, 0.0
        )
        n_full = jnp.sum(full, axis=1, keepdims=True)
        n_edge = jnp.sum(edge, axis=1, keepdims=True)
        full_rank = jnp.dot(full, before, preferred_element_type=jnp.float32)
        edge_rank = jnp.dot(edge, before, preferred_element_type=jnp.float32) + n_full
        slot = jnp.where(full > 0, full_rank, jnp.where(edge > 0, edge_rank, -1.0)).astype(jnp.int32)
        hits = jnp.where(row == jnp.broadcast_to(slot, (count, count)), 1.0, 0.0)
        listed = lax.dot_general(
            (blocks // 16).astype(jnp.float32), hits, (((1,), (1,)), ((), ())), preferred_element_type=jnp.float32
        ) * 16.0 + lax.dot_general(
            (blocks % 16).astype(jnp.float32), hits, (((1,), (1,)), ((), ())), preferred_element_type=jnp.float32
        )
        line = jnp.concatenate(
            [listed, jnp.zeros((1, META - count), jnp.float32)], axis=1
        ).astype(jnp.int32)
        line = jnp.where(lane == count, n_full.astype(jnp.int32), line)
        line = jnp.where(lane == count + 1, (n_full + n_edge).astype(jnp.int32), line)
        line = jnp.where(lane == count + 2, start, line)
        line = jnp.where(lane == count + 3, me, line)
        outs[j][...] = line


def make_lists(rows, turns, flags, me, span_offset, owners, held, tokens):
    smem = pl.BlockSpec(memory_space=pltpu.SMEM)
    vmem = pl.BlockSpec(memory_space=pltpu.VMEM)
    return pl.pallas_call(
        functools.partial(list_kernel, owners, held, tokens, turns, flags),
        out_shape=[jax.ShapeDtypeStruct((1, META), jnp.int32)] * len(turns),
        in_specs=[smem, smem] + [vmem] * len(rows),
        out_specs=[vmem] * len(turns),
        cost_estimate=pl.CostEstimate(flops=1, bytes_accessed=1, transcendentals=0),
    )(me.reshape(1), span_offset, *rows)


def body(queries, latent, selection, span_offset, w_absorb, w_value, w_out):
    owners = lax.axis_size("ctx")
    groups = lax.axis_size("head")
    me = lax.axis_index("ctx")
    column = lax.axis_index("head")
    chips = owners // 2
    depth = 3 * selection.shape[1] // (2 * owners)
    heads = w_absorb.shape[0]
    tokens = queries.shape[0]
    sibling = [(i, i ^ 1) for i in range(owners)]
    turns = range(1, chips)
    ahead = {t: [(i, (i + 2 * t) % owners) for i in range(owners)] for t in turns}
    back = {t: [(i, (i - 2 * t) % owners) for i in range(owners)] for t in turns}
    own = latent.T

    held = latent.shape[0] // BT

    far_queries = {t: lax.ppermute(queries, "ctx", ahead[t]) for t in turns}
    sib = lax.ppermute(own, "ctx", sibling)
    far_rows = {t: lax.ppermute(selection, "ctx", ahead[t]) for t in turns}
    lists = functools.partial(
        make_lists, me=me, span_offset=span_offset, owners=owners, held=held, tokens=tokens
    )
    near_meta, side_meta = lists([selection], [0, 0], [(True, False), (False, True)])
    weights = (w_absorb, w_value)
    whole = [(0, tokens)]
    (near,) = attend(near_meta, queries, own, own, *weights, depth, 1024, whole)
    (side,) = attend(
        side_meta, queries, own, sib, *weights, depth, 1024, whole
    )
    near = combine([near, side], heads, True)
    cuts = [(0, FIRST), (FIRST, tokens)] if chips == 2 else whole
    if chips == 2:
        far_near = lax.ppermute(near, "ctx", ahead[1])
        (meta,) = lists([far_rows[1]], [1], [(True, True)])
        meta, near = lax.optimization_barrier((meta, near))
        fars = attend(meta, far_queries[1], own, sib, *weights, 2 * depth, 1024, cuts)
        *fars, far_near = lax.optimization_barrier((*fars, far_near))
        gots = []
        for far in fars:
            if gots:
                far, gots[-1] = lax.optimization_barrier((far, gots[-1]))
            gots.append(lax.ppermute(far, "ctx", ahead[1]))

        def mine_of(c):
            return settle(near, far_near, fars[c], gots[c], cuts[c][0], heads)
    else:
        arrived = [near]
        for t in turns:
            (meta,) = lists([far_rows[t]], [t], [(True, True)])
            (far,) = attend(meta, far_queries[t], own, sib, *weights, 2 * depth, 1024, whole)
            arrived.append(lax.ppermute(far, "ctx", back[t]))
        mine = combine(arrived, heads, False)
        mine = jnp.concatenate([mine] + [lax.ppermute(mine, "ctx", ahead[t]) for t in turns], axis=0)

        def mine_of(c):
            return mine

    outputs = []
    for c, (low, high) in enumerate(cuts):
        piece = high - low
        mine = mine_of(c)
        shares = project(mine, lax.ppermute(mine, "ctx", sibling), w_out)

        def share_of(block):
            turn = (me // 2 - block // 2) % chips
            place = (me + block) % 2 * chips + turn
            return lax.dynamic_slice_in_dim(shares, place * piece, piece, 0)

        steps = sorted(range(1, groups), key=lambda s: -min(s, groups - s))
        moved = [
            lax.ppermute(
                share_of((column + s) % groups), "head", [(i, (i + s) % groups) for i in range(groups)]
            )
            for s in steps
        ]
        arrived = [share_of(column)] + moved
        outputs.append(sum(a.astype(jnp.float32) for a in arrived).astype(jnp.bfloat16))
    return jnp.concatenate(outputs, axis=0)


def solution(mesh):
    placed = (
        P(("groups", "ctx"), "head"),
        P(("groups", "ctx"), None),
        P(("groups", "ctx"), None),
        P("groups"),
        P("head", None, None),
        P("head", None, None),
        P("head", "ctx"),
    )
    return jax.shard_map(
        body, mesh=mesh, in_specs=placed, out_specs=P(("groups", "head"), "ctx"), check_vma=False
    )
```

```python
import functools
import math

import jax
import jax.numpy as jnp
from jax import lax
from jax.experimental import pallas as pl
from jax.experimental.pallas import tpu as pltpu
from jax.sharding import PartitionSpec as P

BT = 64
WIDE = 128
CHUNK = 8
SMALL = 4
FIRST = 64
NEVER = -1e30
FAR = 1 << 30
MIB = 1024 * 1024
META = 128


def attend_kernel(
    blocks_held, cuts, joined,
    meta, query_hbm, wa_hbm, own_hbm, sib_hbm, wv_hbm, *refs,
):
    earlier, refs = refs[:joined], refs[joined:]
    outs, refs = refs[: len(cuts)], refs[len(cuts) :]
    raw, queries, kt, q_full, wa, wv, *refs = refs
    accs, stores, peaks, totals = refs[0:2], refs[2:4], refs[4:6], refs[6:8]
    wa_sem, wv_sem, q_sem, kv_sem = refs[8:]

    tokens = queries.shape[0]
    heads, nope, lat = wa.shape
    width = kt.shape[0]
    vd = wv.shape[2]
    head_width = nope + width - lat
    fold = head_width ** -0.5 * math.log2(math.e)
    full, count, first, mine = meta[64], meta[65], meta[66], meta[67]
    plain_chunks = full // CHUNK
    done = plain_chunks * CHUNK
    small_chunks = (count - done + SMALL - 1) // SMALL
    slots = done + small_chunks * SMALL

    q_copy = pltpu.make_async_copy(query_hbm, queries, q_sem)
    wa_copy = pltpu.make_async_copy(wa_hbm, wa, wa_sem)
    wv_copy = pltpu.make_async_copy(wv_hbm, wv, wv_sem)
    q_copy.start()
    wa_copy.start()

    def fetch(i, _):
        block = meta[i]
        col = pl.multiple_of((block % blocks_held) // 2 * WIDE, WIDE)
        here = (block // blocks_held == mine) | (i >= count)

        @pl.when(here)
        def _():
            pltpu.make_async_copy(own_hbm.at[:, pl.ds(col, WIDE)], raw.at[i], kv_sem).start()

        @pl.when(jnp.logical_not(here))
        def _():
            pltpu.make_async_copy(sib_hbm.at[:, pl.ds(col, WIDE)], raw.at[i], kv_sem).start()

        return 0

    lax.fori_loop(0, slots, fetch, 0)
    wv_copy.start()
    q_copy.wait()
    wa_copy.wait()
    for h in range(heads):
        base = h * head_width
        latent_part = jnp.dot(
            queries[:, base : base + nope], wa[h], preferred_element_type=jnp.float32
        )
        rows = slice(h * tokens, (h + 1) * tokens)
        q_full[rows, 0:lat] = (latent_part * fold).astype(jnp.bfloat16)
        turned = queries[:, base + nope : base + head_width].astype(jnp.float32)
        q_full[rows, lat:width] = (turned * fold).astype(jnp.bfloat16)

    def land(i, _):
        pltpu.make_async_copy(own_hbm.at[:, pl.ds(0, WIDE)], raw.at[0], kv_sem).wait()
        return 0

    lax.fori_loop(0, slots, land, 0)

    def pair(i, _):
        left_odd = meta[2 * i] % 2 == 1
        right_odd = meta[2 * i + 1] % 2 == 1
        target = pl.ds(pl.multiple_of(i * WIDE, WIDE), WIDE)
        lane = lax.broadcasted_iota(jnp.int32, (width, WIDE), 1)

        def swap(x):
            return jnp.concatenate([x[:, BT:], x[:, :BT]], axis=1)

        @pl.when(jnp.logical_not(left_odd) & right_odd)
        def _():
            kt[:, target] = jnp.where(lane < BT, raw[2 * i], raw[2 * i + 1])

        @pl.when(left_odd & right_odd)
        def _():
            kt[:, target] = jnp.where(lane < BT, swap(raw[2 * i]), raw[2 * i + 1])

        @pl.when(jnp.logical_not(left_odd | right_odd))
        def _():
            kt[:, target] = jnp.where(lane < BT, raw[2 * i], swap(raw[2 * i + 1]))

        @pl.when(left_odd & jnp.logical_not(right_odd))
        def _():
            kt[:, target] = swap(jnp.where(lane < BT, raw[2 * i + 1], raw[2 * i]))

        return 0

    lax.fori_loop(0, slots // 2, pair, 0)
    wv_copy.wait()

    tile = accs[0].shape[0]
    tile_heads = tile // tokens
    lane = lax.broadcasted_iota(jnp.int32, (tokens, 128), 1)

    def row_pair(r, lse_tile):
        row0 = r * 2 * tile
        bases = [pl.multiple_of(row0, tile), pl.multiple_of(row0 + tile, tile)]
        for i in range(2):
            accs[i][...] = jnp.zeros_like(accs[i])
            peaks[i][...] = jnp.full(peaks[i].shape, NEVER, jnp.float32)
            totals[i][...] = jnp.zeros_like(totals[i])

        def score(i, key0, n):
            stores[i][:, 0 : n * BT] = jnp.dot(
                q_full[pl.ds(bases[i], tile), :], kt[:, pl.ds(key0, n * BT)],
                preferred_element_type=jnp.float32,
            )

        def soften(i, n, visible):
            scores = stores[i][:, 0 : n * BT]
            if visible is not None:
                scores = jnp.where(
                    visible[None], scores.reshape(tile_heads, tokens, n * BT), NEVER
                ).reshape(tile, n * BT)
            peak = peaks[i][...]
            new_peak = jnp.maximum(peak, jnp.max(scores, axis=1, keepdims=True))
            peaks[i][...] = new_peak
            raised = jnp.exp2(scores - new_peak[:, 0:1])
            keep_share = jnp.exp2(peak - new_peak)
            total = totals[i][...] * keep_share
            for k in range(n * BT // 128):
                total = total + raised[:, k * 128 : (k + 1) * 128]
            totals[i][...] = total
            return raised.astype(jnp.bfloat16), keep_share[:, 0:1]

        def mix(i, key0, n, raised, keep_share):
            accs[i][...] = accs[i][...] * keep_share + lax.dot_general(
                raised, kt[0:lat, pl.ds(key0, n * BT)], (((1,), (1,)), ((), ())),
                preferred_element_type=jnp.float32,
            )

        def chunk(n, start, masked, c, _):
            key0 = pl.multiple_of(start + c * n * BT, 128)
            key1 = pl.multiple_of(key0 + n * BT, 128)
            visible = None
            if masked:
                block0 = key0 // BT
                column = lax.broadcasted_iota(jnp.int32, (tokens, n * BT), 1)
                position = jnp.zeros((tokens, n * BT), jnp.int32)
                for b in range(n):
                    at = jnp.where(
                        block0 + b < full, 0,
                        jnp.where(block0 + b < count, meta[block0 + b] * BT, FAR),
                    )
                    position = jnp.where(column // BT == b, at + column % BT, position)
                query = first + lax.broadcasted_iota(jnp.int32, (tokens, n * BT), 0)
                visible = position <= query
            score(1, key0, n)
            raised, share = soften(0, n, visible)
            mix(0, key0, n, raised, share)
            score(0, key1, n)
            raised, share = soften(1, n, visible)
            mix(1, key0, n, raised, share)
            return 0

        @pl.when(plain_chunks > 0)
        def _():
            score(0, 0, CHUNK)

        @pl.when(plain_chunks == 0)
        def _():
            score(0, 0, SMALL)

        lax.fori_loop(0, plain_chunks, functools.partial(chunk, CHUNK, 0, False), 0)
        lax.fori_loop(0, small_chunks, functools.partial(chunk, SMALL, done * BT, True), 0)

        for i in range(2):
            total = jnp.maximum(jnp.sum(totals[i][...], axis=1, keepdims=True), 1e-30)
            lse = peaks[i][:, 0:1] + jnp.log2(total)
            scale = 1.0 / total
            for k in range(tile_heads):
                h = (r * 2 + i) * tile_heads + k
                rows = slice(k * tokens, (k + 1) * tokens)
                mixed = (accs[i][rows, :] * scale[rows, :]).astype(jnp.bfloat16)
                out = jnp.dot(mixed, wv[h], preferred_element_type=jnp.float32)
                out = out.astype(jnp.bfloat16)
                for ref, (low, high) in zip(outs, cuts):
                    ref[:, pl.ds(pl.multiple_of(h * vd, vd), vd)] = out[low:high, :]
                lse_tile = place_log(lse_tile, lane, h, lse[rows, :])
        return lse_tile

    lse_tile = lax.fori_loop(
        0, heads * tokens // (2 * tile), row_pair, jnp.zeros((tokens, 128), jnp.float32)
    ).astype(jnp.bfloat16)
    for ref, (low, high) in zip(outs, cuts):
        ref[:, heads * vd :] = lse_tile[low:high, :]
        if joined:
            parts = [(earlier[0], slice(low, high)), (ref, slice(0, high - low))]
            merge(parts, heads, ref, slice(0, high - low), True)


def place_log(tile, lane, h, value):
    high = value.astype(jnp.bfloat16).astype(jnp.float32)
    middle = (value - high).astype(jnp.bfloat16).astype(jnp.float32)
    low = value - high - middle
    tile = jnp.where(lane == h, high, tile)
    tile = jnp.where(lane == h + 32, middle, tile)
    return jnp.where(lane == h + 64, low, tile)


def attend(meta, queries, own, sib, w_absorb, w_value, slots, row_tile, cuts, *earlier):
    tokens = queries.shape[0]
    heads, nope, lat = w_absorb.shape
    vd = w_value.shape[2]
    width = own.shape[0]
    slots = -(-slots // SMALL) * SMALL
    rows = heads * tokens
    tile = min(row_tile, rows // 2)
    keys = slots * BT * 2 // 3
    any_space = pl.BlockSpec(memory_space=pl.ANY)
    vmem = pl.BlockSpec(memory_space=pltpu.VMEM)
    smem = pl.BlockSpec(memory_space=pltpu.SMEM)
    return pl.pallas_call(
        functools.partial(attend_kernel, own.shape[1] // BT, cuts, len(earlier)),
        out_shape=[
            jax.ShapeDtypeStruct((high - low, heads * vd + 128), jnp.bfloat16) for low, high in cuts
        ],
        in_specs=[smem] + [any_space] * 5 + [vmem] * len(earlier),
        out_specs=[vmem] * len(cuts),
        scratch_shapes=[
            pltpu.VMEM((slots, width, WIDE), jnp.bfloat16),
            pltpu.VMEM(queries.shape, jnp.bfloat16),
            pltpu.VMEM((width, (slots + CHUNK) * BT), jnp.bfloat16),
            pltpu.VMEM((rows, width), jnp.bfloat16),
            pltpu.VMEM(w_absorb.shape, jnp.bfloat16),
            pltpu.VMEM(w_value.shape, jnp.bfloat16),
            *[pltpu.VMEM((tile, lat), jnp.float32)] * 2,
            *[pltpu.VMEM((tile, CHUNK * BT), jnp.float32)] * 2,
            *[pltpu.VMEM((tile, 128), jnp.float32)] * 4,
            *[pltpu.SemaphoreType.DMA] * 4,
        ],
        compiler_params=pltpu.CompilerParams(vmem_limit_bytes=50 * MIB),
        cost_estimate=pl.CostEstimate(
            flops=2 * rows * keys * (width + lat),
            bytes_accessed=2 * keys * width * 2,
            transcendentals=rows * keys,
        ),
    )(meta.reshape(-1), queries, w_absorb, own, sib, w_value, *earlier)


def read_log(ref, rows, heads):
    tail = ref[rows, ref.shape[1] - 128 :].astype(jnp.float32)
    return tail[:, 0:heads] + tail[:, 32 : 32 + heads] + tail[:, 64 : 64 + heads]


def merge(parts, heads, out, out_rows, with_log):
    vd = (parts[0][0].shape[1] - 128) // heads
    logs = [read_log(ref, rows, heads) for ref, rows in parts]
    peak = functools.reduce(jnp.maximum, logs)
    shares = [jnp.exp2(value - peak) for value in logs]
    total = functools.reduce(jnp.add, shares)
    norm = 1.0 / total
    for h in range(heads):
        columns = slice(h * vd, (h + 1) * vd)
        mixed = sum(
            ref[rows, columns].astype(jnp.float32) * (share * norm)[:, h : h + 1]
            for (ref, rows), share in zip(parts, shares)
        )
        out[out_rows, columns] = mixed.astype(jnp.bfloat16)
    if with_log:
        log = peak + jnp.log2(total)
        tokens = log.shape[0]
        lane = lax.broadcasted_iota(jnp.int32, (tokens, 128), 1)
        tile = jnp.zeros((tokens, 128), jnp.float32)
        for h in range(heads):
            tile = place_log(tile, lane, h, log[:, h : h + 1])
        out[out_rows, heads * vd :] = tile.astype(jnp.bfloat16)


def small_call(kernel, shape, operands):
    vmem = pl.BlockSpec(memory_space=pltpu.VMEM)
    return pl.pallas_call(
        kernel,
        out_shape=jax.ShapeDtypeStruct(shape, jnp.bfloat16),
        in_specs=[vmem] * len(operands),
        out_specs=vmem,
        compiler_params=pltpu.CompilerParams(vmem_limit_bytes=16 * MIB),
        cost_estimate=pl.CostEstimate(flops=1, bytes_accessed=1, transcendentals=0),
    )(*operands)


def combine(partials, heads):
    tokens, columns = partials[0].shape

    def kernel(*refs):
        rows = slice(0, tokens)
        merge([(ref, rows) for ref in refs[:-1]], heads, refs[-1], rows, False)

    return small_call(kernel, (tokens, columns - 128), partials)


def settle(near, far_near, far, got, low, heads):
    rows, columns = far.shape
    cut, whole = slice(low, low + rows), slice(0, rows)

    def kernel(near_ref, far_near_ref, far_ref, got_ref, out):
        merge([(near_ref, cut), (got_ref, whole)], heads, out, whole, False)
        merge([(far_near_ref, cut), (far_ref, whole)], heads, out, slice(rows, 2 * rows), False)

    return small_call(kernel, (2 * rows, columns - 128), [near, far_near, far, got])


def project_kernel(steps, mine_ref, other_ref, w_hbm, o_ref, w, acc, sems):
    depth = w.shape[0] // steps
    copies = [
        pltpu.make_async_copy(w_hbm.at[k * depth : (k + 1) * depth, :], w.at[k * depth : (k + 1) * depth, :], sems.at[k])
        for k in range(steps)
    ]
    for copy in copies:
        copy.start()
    for k, copy in enumerate(copies):
        rows = slice(k * depth, (k + 1) * depth)
        x = jnp.concatenate([mine_ref[:, rows], other_ref[:, rows]], axis=0)
        copy.wait()
        part = jnp.dot(x, w[rows, :], preferred_element_type=jnp.float32)
        if k > 0:
            part = acc[...] + part
        if k < steps - 1:
            acc[...] = part
        else:
            o_ref[...] = part.astype(jnp.bfloat16)


def project(mine, other, w):
    rows, depth = mine.shape
    columns = w.shape[1]
    steps = 4
    vmem = pl.BlockSpec(memory_space=pltpu.VMEM)
    return pl.pallas_call(
        functools.partial(project_kernel, steps),
        out_shape=jax.ShapeDtypeStruct((2 * rows, columns), jnp.bfloat16),
        in_specs=[vmem, vmem, pl.BlockSpec(memory_space=pltpu.HBM)],
        out_specs=vmem,
        scratch_shapes=[
            pltpu.VMEM(w.shape, jnp.bfloat16),
            pltpu.VMEM((2 * rows, columns), jnp.float32),
            pltpu.SemaphoreType.DMA((steps,)),
        ],
        compiler_params=pltpu.CompilerParams(vmem_limit_bytes=50 * MIB),
        cost_estimate=pl.CostEstimate(flops=1, bytes_accessed=1, transcendentals=0),
    )(mine, other, w)


def list_kernel(owners, held, tokens, turns, flags, me_ref, offset_ref, *refs):
    outs = refs[-len(turns) :]
    refs = refs[: -len(turns)]
    me = me_ref[0]
    count = refs[0].shape[1]
    row = lax.broadcasted_iota(jnp.int32, (count, count), 0)
    col = lax.broadcasted_iota(jnp.int32, (count, count), 1)
    before = (row < col).astype(jnp.float32)
    lane = lax.broadcasted_iota(jnp.int32, (1, META), 1)
    for j, turn in enumerate(turns):
        blocks = refs[j][...]
        start = offset_ref[0] + lax.rem(me - 2 * turn + owners, owners) * tokens
        here = jnp.zeros(blocks.shape, jnp.bool_)
        for wanted, holder in zip(flags[j], (me, me ^ 1)):
            if wanted:
                here = here | ((blocks >= holder * held) & (blocks < (holder + 1) * held))
        seen = blocks * BT + (BT - 1) <= start
        full = jnp.where(here & seen, 1.0, 0.0)
        edge = jnp.where(
            here & jnp.logical_not(seen) & (blocks * BT <= start + tokens - 1), 1.0, 0.0
        )
        n_full = jnp.sum(full, axis=1, keepdims=True)
        n_edge = jnp.sum(edge, axis=1, keepdims=True)
        full_rank = jnp.dot(full, before, preferred_element_type=jnp.float32)
        edge_rank = jnp.dot(edge, before, preferred_element_type=jnp.float32) + n_full
        slot = jnp.where(full > 0, full_rank, jnp.where(edge > 0, edge_rank, -1.0)).astype(jnp.int32)
        hits = jnp.where(row == jnp.broadcast_to(slot, (count, count)), 1.0, 0.0)
        listed = lax.dot_general(
            (blocks // 16).astype(jnp.float32), hits, (((1,), (1,)), ((), ())), preferred_element_type=jnp.float32
        ) * 16.0 + lax.dot_general(
            (blocks % 16).astype(jnp.float32), hits, (((1,), (1,)), ((), ())), preferred_element_type=jnp.float32
        )
        line = jnp.concatenate(
            [listed, jnp.zeros((1, META - count), jnp.float32)], axis=1
        ).astype(jnp.int32)
        line = jnp.where(lane == count, n_full.astype(jnp.int32), line)
        line = jnp.where(lane == count + 1, (n_full + n_edge).astype(jnp.int32), line)
        line = jnp.where(lane == count + 2, start, line)
        line = jnp.where(lane == count + 3, me, line)
        outs[j][...] = line


def make_lists(rows, turns, flags, me, span_offset, owners, held, tokens):
    smem = pl.BlockSpec(memory_space=pltpu.SMEM)
    vmem = pl.BlockSpec(memory_space=pltpu.VMEM)
    return pl.pallas_call(
        functools.partial(list_kernel, owners, held, tokens, turns, flags),
        out_shape=[jax.ShapeDtypeStruct((1, META), jnp.int32)] * len(turns),
        in_specs=[smem, smem] + [vmem] * len(rows),
        out_specs=[vmem] * len(turns),
        cost_estimate=pl.CostEstimate(flops=1, bytes_accessed=1, transcendentals=0),
    )(me.reshape(1), span_offset, *rows)


def body(queries, latent, selection, span_offset, w_absorb, w_value, w_out):
    owners = lax.axis_size("ctx")
    groups = lax.axis_size("head")
    me = lax.axis_index("ctx")
    column = lax.axis_index("head")
    chips = owners // 2
    depth = 3 * selection.shape[1] // (2 * owners)
    heads = w_absorb.shape[0]
    tokens = queries.shape[0]
    sibling = [(i, i ^ 1) for i in range(owners)]
    turns = range(1, chips)
    ahead = {t: [(i, (i + 2 * t) % owners) for i in range(owners)] for t in turns}
    back = {t: [(i, (i - 2 * t) % owners) for i in range(owners)] for t in turns}
    own = latent.T

    held = latent.shape[0] // BT

    far_queries = {t: lax.ppermute(queries, "ctx", ahead[t]) for t in turns}
    sib = lax.ppermute(own, "ctx", sibling)
    far_rows = {t: lax.ppermute(selection, "ctx", ahead[t]) for t in turns}
    lists = functools.partial(
        make_lists, me=me, span_offset=span_offset, owners=owners, held=held, tokens=tokens
    )
    near_meta, side_meta, *far_metas = lists(
        [selection, selection] + [far_rows[t] for t in turns],
        [0, 0, *turns],
        [(True, False), (False, True)] + [(True, True)] * (chips - 1),
    )
    weights = (w_absorb, w_value)
    whole = [(0, tokens)]
    (near,) = attend(near_meta, queries, own, own, *weights, depth, 1024, whole)
    (near,) = attend(side_meta, queries, own, sib, *weights, depth, 1024, whole, near)
    cuts = [(0, FIRST), (FIRST, tokens)] if chips == 2 else whole
    if chips == 2:
        far_near = lax.ppermute(near, "ctx", ahead[1])
        meta, near = lax.optimization_barrier((far_metas[0], near))
        fars = attend(meta, far_queries[1], own, sib, *weights, 2 * depth, 1024, cuts)
        *fars, far_near = lax.optimization_barrier((*fars, far_near))
        gots = []
        for far in fars:
            if gots:
                far, gots[-1] = lax.optimization_barrier((far, gots[-1]))
            gots.append(lax.ppermute(far, "ctx", ahead[1]))

        def mine_of(c, last):
            got, *_ = lax.optimization_barrier((gots[c], *last))
            return settle(near, far_near, fars[c], got, cuts[c][0], heads)
    else:
        arrived = [near]
        for t in turns:
            (far,) = attend(far_metas[t - 1], far_queries[t], own, sib, *weights, 2 * depth, 1024, whole)
            arrived.append(lax.ppermute(far, "ctx", back[t]))
        mine = combine(arrived, heads)
        mine = jnp.concatenate([mine] + [lax.ppermute(mine, "ctx", ahead[t]) for t in turns], axis=0)

        def mine_of(c, last):
            return mine

    outputs, last = [], []
    for c, (low, high) in enumerate(cuts):
        piece = high - low
        mine = mine_of(c, last)
        shares = project(mine, lax.ppermute(mine, "ctx", sibling), w_out)

        def share_of(block):
            turn = (me // 2 - block // 2) % chips
            place = (me + block) % 2 * chips + turn
            return lax.dynamic_slice_in_dim(shares, place * piece, piece, 0)

        steps = sorted(range(1, groups), key=lambda s: -min(s, groups - s))
        moved = [
            lax.ppermute(
                share_of((column + s) % groups), "head", [(i, (i + s) % groups) for i in range(groups)]
            )
            for s in steps
        ]
        last = [shares]
        arrived = [share_of(column)] + moved
        outputs.append(sum(a.astype(jnp.float32) for a in arrived).astype(jnp.bfloat16))
    return jnp.concatenate(outputs, axis=0)


def solution(mesh):
    placed = (
        P(("groups", "ctx"), "head"),
        P(("groups", "ctx"), None),
        P(("groups", "ctx"), None),
        P("groups"),
        P("head", None, None),
        P("head", None, None),
        P("head", "ctx"),
    )
    return jax.shard_map(
        body, mesh=mesh, in_specs=placed, out_specs=P(("groups", "head"), "ctx"), check_vma=False
    )
```

```python
import functools
import math

import jax
import jax.numpy as jnp
from jax import lax
from jax.experimental import pallas as pl
from jax.experimental.pallas import tpu as pltpu
from jax.sharding import PartitionSpec as P

BT = 64
WIDE = 128
CHUNK = 8
SMALL = 4
FIRST = 64
NEVER = -1e30
FAR = 1 << 30
MIB = 1024 * 1024
META = 128


def attend_kernel(
    blocks_held, cuts, joined,
    meta, query_hbm, wa_hbm, own_hbm, sib_hbm, wv_hbm, *refs,
):
    earlier, refs = refs[:joined], refs[joined:]
    outs, refs = refs[: len(cuts)], refs[len(cuts) :]
    raw, queries, kt, q_full, wa, wv, *refs = refs
    accs, stores, peaks, totals = refs[0:2], refs[2:4], refs[4:6], refs[6:8]
    wa_sem, wv_sem, q_sem, kv_sem = refs[8:]

    tokens = queries.shape[0]
    heads, nope, lat = wa.shape
    width = kt.shape[0]
    vd = wv.shape[2]
    head_width = nope + width - lat
    fold = head_width ** -0.5 * math.log2(math.e)
    full, count, first, mine = meta[64], meta[65], meta[66], meta[67]
    plain_chunks = full // CHUNK
    done = plain_chunks * CHUNK
    small_chunks = (count - done + SMALL - 1) // SMALL
    slots = done + small_chunks * SMALL

    q_copy = pltpu.make_async_copy(query_hbm, queries, q_sem)
    wa_copy = pltpu.make_async_copy(wa_hbm, wa, wa_sem)
    wv_copy = pltpu.make_async_copy(wv_hbm, wv, wv_sem)
    q_copy.start()
    wa_copy.start()

    def fetch(i, _):
        block = meta[i]
        col = pl.multiple_of((block % blocks_held) // 2 * WIDE, WIDE)
        here = (block // blocks_held == mine) | (i >= count)

        @pl.when(here)
        def _():
            pltpu.make_async_copy(own_hbm.at[:, pl.ds(col, WIDE)], raw.at[i], kv_sem).start()

        @pl.when(jnp.logical_not(here))
        def _():
            pltpu.make_async_copy(sib_hbm.at[:, pl.ds(col, WIDE)], raw.at[i], kv_sem).start()

        return 0

    lax.fori_loop(0, slots, fetch, 0)
    wv_copy.start()
    q_copy.wait()
    wa_copy.wait()
    for h in range(heads):
        base = h * head_width
        latent_part = jnp.dot(
            queries[:, base : base + nope], wa[h], preferred_element_type=jnp.float32
        )
        rows = slice(h * tokens, (h + 1) * tokens)
        q_full[rows, 0:lat] = (latent_part * fold).astype(jnp.bfloat16)
        turned = queries[:, base + nope : base + head_width].astype(jnp.float32)
        q_full[rows, lat:width] = (turned * fold).astype(jnp.bfloat16)

    def land(i, _):
        pltpu.make_async_copy(own_hbm.at[:, pl.ds(0, WIDE)], raw.at[0], kv_sem).wait()
        return 0

    lax.fori_loop(0, slots, land, 0)

    def pair(i, _):
        left_odd = meta[2 * i] % 2 == 1
        right_odd = meta[2 * i + 1] % 2 == 1
        target = pl.ds(pl.multiple_of(i * WIDE, WIDE), WIDE)
        lane = lax.broadcasted_iota(jnp.int32, (width, WIDE), 1)

        def swap(x):
            return jnp.concatenate([x[:, BT:], x[:, :BT]], axis=1)

        @pl.when(jnp.logical_not(left_odd) & right_odd)
        def _():
            kt[:, target] = jnp.where(lane < BT, raw[2 * i], raw[2 * i + 1])

        @pl.when(left_odd & right_odd)
        def _():
            kt[:, target] = jnp.where(lane < BT, swap(raw[2 * i]), raw[2 * i + 1])

        @pl.when(jnp.logical_not(left_odd | right_odd))
        def _():
            kt[:, target] = jnp.where(lane < BT, raw[2 * i], swap(raw[2 * i + 1]))

        @pl.when(left_odd & jnp.logical_not(right_odd))
        def _():
            kt[:, target] = swap(jnp.where(lane < BT, raw[2 * i + 1], raw[2 * i]))

        return 0

    lax.fori_loop(0, slots // 2, pair, 0)
    wv_copy.wait()

    tile = accs[0].shape[0]
    tile_heads = tile // tokens
    lane = lax.broadcasted_iota(jnp.int32, (tokens, 128), 1)

    def row_pair(r, lse_tile):
        row0 = r * 2 * tile
        bases = [pl.multiple_of(row0, tile), pl.multiple_of(row0 + tile, tile)]
        for i in range(2):
            accs[i][...] = jnp.zeros_like(accs[i])
            peaks[i][...] = jnp.full(peaks[i].shape, NEVER, jnp.float32)
            totals[i][...] = jnp.zeros_like(totals[i])

        def score(i, key0, n):
            stores[i][:, 0 : n * BT] = jnp.dot(
                q_full[pl.ds(bases[i], tile), :], kt[:, pl.ds(key0, n * BT)],
                preferred_element_type=jnp.float32,
            )

        def soften(i, n, visible):
            scores = stores[i][:, 0 : n * BT]
            if visible is not None:
                scores = jnp.where(
                    visible[None], scores.reshape(tile_heads, tokens, n * BT), NEVER
                ).reshape(tile, n * BT)
            peak = peaks[i][...]
            new_peak = jnp.maximum(peak, jnp.max(scores, axis=1, keepdims=True))
            peaks[i][...] = new_peak
            raised = jnp.exp2(scores - new_peak[:, 0:1])
            keep_share = jnp.exp2(peak - new_peak)
            total = totals[i][...] * keep_share
            for k in range(n * BT // 128):
                total = total + raised[:, k * 128 : (k + 1) * 128]
            totals[i][...] = total
            return raised.astype(jnp.bfloat16), keep_share[:, 0:1]

        def mix(i, key0, n, raised, keep_share):
            accs[i][...] = accs[i][...] * keep_share + lax.dot_general(
                raised, kt[0:lat, pl.ds(key0, n * BT)], (((1,), (1,)), ((), ())),
                preferred_element_type=jnp.float32,
            )

        def chunk(n, start, masked, c, _):
            key0 = pl.multiple_of(start + c * n * BT, 128)
            key1 = pl.multiple_of(key0 + n * BT, 128)
            visible = None
            if masked:
                block0 = key0 // BT
                column = lax.broadcasted_iota(jnp.int32, (tokens, n * BT), 1)
                position = jnp.zeros((tokens, n * BT), jnp.int32)
                for b in range(n):
                    at = jnp.where(
                        block0 + b < full, 0,
                        jnp.where(block0 + b < count, meta[block0 + b] * BT, FAR),
                    )
                    position = jnp.where(column // BT == b, at + column % BT, position)
                query = first + lax.broadcasted_iota(jnp.int32, (tokens, n * BT), 0)
                visible = position <= query
            score(1, key0, n)
            raised, share = soften(0, n, visible)
            mix(0, key0, n, raised, share)
            score(0, key1, n)
            raised, share = soften(1, n, visible)
            mix(1, key0, n, raised, share)
            return 0

        @pl.when(plain_chunks > 0)
        def _():
            score(0, 0, CHUNK)

        @pl.when(plain_chunks == 0)
        def _():
            score(0, 0, SMALL)

        lax.fori_loop(0, plain_chunks, functools.partial(chunk, CHUNK, 0, False), 0)
        lax.fori_loop(0, small_chunks, functools.partial(chunk, SMALL, done * BT, True), 0)

        for i in range(2):
            total = jnp.maximum(jnp.sum(totals[i][...], axis=1, keepdims=True), 1e-30)
            lse = peaks[i][:, 0:1] + jnp.log2(total)
            scale = 1.0 / total
            for k in range(tile_heads):
                h = (r * 2 + i) * tile_heads + k
                rows = slice(k * tokens, (k + 1) * tokens)
                mixed = (accs[i][rows, :] * scale[rows, :]).astype(jnp.bfloat16)
                out = jnp.dot(mixed, wv[h], preferred_element_type=jnp.float32)
                out = out.astype(jnp.bfloat16)
                for ref, (low, high) in zip(outs, cuts):
                    ref[:, pl.ds(pl.multiple_of(h * vd, vd), vd)] = out[low:high, :]
                lse_tile = place_log(lse_tile, lane, h, lse[rows, :])
        return lse_tile

    lse_tile = lax.fori_loop(
        0, heads * tokens // (2 * tile), row_pair, jnp.zeros((tokens, 128), jnp.float32)
    ).astype(jnp.bfloat16)
    for ref, (low, high) in zip(outs, cuts):
        ref[:, heads * vd :] = lse_tile[low:high, :]
        if joined:
            parts = [(earlier[0], slice(low, high)), (ref, slice(0, high - low))]
            merge(parts, heads, ref, slice(0, high - low), True)


def place_log(tile, lane, h, value):
    high = value.astype(jnp.bfloat16).astype(jnp.float32)
    middle = (value - high).astype(jnp.bfloat16).astype(jnp.float32)
    low = value - high - middle
    tile = jnp.where(lane == h, high, tile)
    tile = jnp.where(lane == h + 32, middle, tile)
    return jnp.where(lane == h + 64, low, tile)


def attend(meta, queries, own, sib, w_absorb, w_value, slots, row_tile, cuts, *earlier):
    tokens = queries.shape[0]
    heads, nope, lat = w_absorb.shape
    vd = w_value.shape[2]
    width = own.shape[0]
    slots = -(-slots // SMALL) * SMALL
    rows = heads * tokens
    tile = min(row_tile, rows // 2)
    keys = slots * BT * 2 // 3
    any_space = pl.BlockSpec(memory_space=pl.ANY)
    vmem = pl.BlockSpec(memory_space=pltpu.VMEM)
    smem = pl.BlockSpec(memory_space=pltpu.SMEM)
    return pl.pallas_call(
        functools.partial(attend_kernel, own.shape[1] // BT, cuts, len(earlier)),
        out_shape=[
            jax.ShapeDtypeStruct((high - low, heads * vd + 128), jnp.bfloat16) for low, high in cuts
        ],
        in_specs=[smem] + [any_space] * 5 + [vmem] * len(earlier),
        out_specs=[vmem] * len(cuts),
        scratch_shapes=[
            pltpu.VMEM((slots, width, WIDE), jnp.bfloat16),
            pltpu.VMEM(queries.shape, jnp.bfloat16),
            pltpu.VMEM((width, (slots + CHUNK) * BT), jnp.bfloat16),
            pltpu.VMEM((rows, width), jnp.bfloat16),
            pltpu.VMEM(w_absorb.shape, jnp.bfloat16),
            pltpu.VMEM(w_value.shape, jnp.bfloat16),
            *[pltpu.VMEM((tile, lat), jnp.float32)] * 2,
            *[pltpu.VMEM((tile, CHUNK * BT), jnp.float32)] * 2,
            *[pltpu.VMEM((tile, 128), jnp.float32)] * 4,
            *[pltpu.SemaphoreType.DMA] * 4,
        ],
        compiler_params=pltpu.CompilerParams(vmem_limit_bytes=50 * MIB),
        cost_estimate=pl.CostEstimate(
            flops=2 * rows * keys * (width + lat),
            bytes_accessed=2 * keys * width * 2,
            transcendentals=rows * keys,
        ),
    )(meta.reshape(-1), queries, w_absorb, own, sib, w_value, *earlier)


def read_log(ref, rows, heads):
    tail = ref[rows, ref.shape[1] - 128 :].astype(jnp.float32)
    return tail[:, 0:heads] + tail[:, 32 : 32 + heads] + tail[:, 64 : 64 + heads]


def merge(parts, heads, out, out_rows, with_log):
    vd = (parts[0][0].shape[1] - 128) // heads
    logs = [read_log(ref, rows, heads) for ref, rows in parts]
    peak = functools.reduce(jnp.maximum, logs)
    shares = [jnp.exp2(value - peak) for value in logs]
    total = functools.reduce(jnp.add, shares)
    norm = 1.0 / total
    for h in range(heads):
        columns = slice(h * vd, (h + 1) * vd)
        mixed = sum(
            ref[rows, columns].astype(jnp.float32) * (share * norm)[:, h : h + 1]
            for (ref, rows), share in zip(parts, shares)
        )
        out[out_rows, columns] = mixed.astype(jnp.bfloat16)
    if with_log:
        log = peak + jnp.log2(total)
        tokens = log.shape[0]
        lane = lax.broadcasted_iota(jnp.int32, (tokens, 128), 1)
        tile = jnp.zeros((tokens, 128), jnp.float32)
        for h in range(heads):
            tile = place_log(tile, lane, h, log[:, h : h + 1])
        out[out_rows, heads * vd :] = tile.astype(jnp.bfloat16)


def small_call(kernel, shape, operands):
    vmem = pl.BlockSpec(memory_space=pltpu.VMEM)
    return pl.pallas_call(
        kernel,
        out_shape=jax.ShapeDtypeStruct(shape, jnp.bfloat16),
        in_specs=[vmem] * len(operands),
        out_specs=vmem,
        compiler_params=pltpu.CompilerParams(vmem_limit_bytes=16 * MIB),
        cost_estimate=pl.CostEstimate(flops=1, bytes_accessed=1, transcendentals=0),
    )(*operands)


def combine(partials, heads):
    tokens, columns = partials[0].shape

    def kernel(*refs):
        rows = slice(0, tokens)
        merge([(ref, rows) for ref in refs[:-1]], heads, refs[-1], rows, False)

    return small_call(kernel, (tokens, columns - 128), partials)


def settle(near, far_near, far, got, low, heads):
    rows, columns = far.shape
    cut, whole = slice(low, low + rows), slice(0, rows)

    def kernel(near_ref, far_near_ref, far_ref, got_ref, out):
        merge([(near_ref, cut), (got_ref, whole)], heads, out, whole, False)
        merge([(far_near_ref, cut), (far_ref, whole)], heads, out, slice(rows, 2 * rows), False)

    return small_call(kernel, (2 * rows, columns - 128), [near, far_near, far, got])


def project_kernel(steps, mine_ref, other_ref, w_hbm, o_ref, w, acc, sems):
    depth = w.shape[0] // steps
    copies = [
        pltpu.make_async_copy(w_hbm.at[k * depth : (k + 1) * depth, :], w.at[k * depth : (k + 1) * depth, :], sems.at[k])
        for k in range(steps)
    ]
    for copy in copies:
        copy.start()
    for k, copy in enumerate(copies):
        rows = slice(k * depth, (k + 1) * depth)
        x = jnp.concatenate([mine_ref[:, rows], other_ref[:, rows]], axis=0)
        copy.wait()
        part = jnp.dot(x, w[rows, :], preferred_element_type=jnp.float32)
        if k > 0:
            part = acc[...] + part
        if k < steps - 1:
            acc[...] = part
        else:
            o_ref[...] = part.astype(jnp.bfloat16)


def project(mine, other, w):
    rows, depth = mine.shape
    columns = w.shape[1]
    steps = 4
    vmem = pl.BlockSpec(memory_space=pltpu.VMEM)
    return pl.pallas_call(
        functools.partial(project_kernel, steps),
        out_shape=jax.ShapeDtypeStruct((2 * rows, columns), jnp.bfloat16),
        in_specs=[vmem, vmem, pl.BlockSpec(memory_space=pltpu.HBM)],
        out_specs=vmem,
        scratch_shapes=[
            pltpu.VMEM(w.shape, jnp.bfloat16),
            pltpu.VMEM((2 * rows, columns), jnp.float32),
            pltpu.SemaphoreType.DMA((steps,)),
        ],
        compiler_params=pltpu.CompilerParams(vmem_limit_bytes=50 * MIB),
        cost_estimate=pl.CostEstimate(flops=1, bytes_accessed=1, transcendentals=0),
    )(mine, other, w)


def list_kernel(owners, held, tokens, turns, flags, me_ref, offset_ref, *refs):
    outs = refs[-len(turns) :]
    refs = refs[: -len(turns)]
    me = me_ref[0]
    count = refs[0].shape[1]
    row = lax.broadcasted_iota(jnp.int32, (count, count), 0)
    col = lax.broadcasted_iota(jnp.int32, (count, count), 1)
    before = (row < col).astype(jnp.float32)
    lane = lax.broadcasted_iota(jnp.int32, (1, META), 1)
    for j, turn in enumerate(turns):
        blocks = refs[j][...]
        start = offset_ref[0] + lax.rem(me - 2 * turn + owners, owners) * tokens
        here = jnp.zeros(blocks.shape, jnp.bool_)
        for wanted, holder in zip(flags[j], (me, me ^ 1)):
            if wanted:
                here = here | ((blocks >= holder * held) & (blocks < (holder + 1) * held))
        seen = blocks * BT + (BT - 1) <= start
        full = jnp.where(here & seen, 1.0, 0.0)
        edge = jnp.where(
            here & jnp.logical_not(seen) & (blocks * BT <= start + tokens - 1), 1.0, 0.0
        )
        n_full = jnp.sum(full, axis=1, keepdims=True)
        n_edge = jnp.sum(edge, axis=1, keepdims=True)
        full_rank = jnp.dot(full, before, preferred_element_type=jnp.float32)
        edge_rank = jnp.dot(edge, before, preferred_element_type=jnp.float32) + n_full
        slot = jnp.where(full > 0, full_rank, jnp.where(edge > 0, edge_rank, -1.0)).astype(jnp.int32)
        hits = jnp.where(row == jnp.broadcast_to(slot, (count, count)), 1.0, 0.0)
        listed = lax.dot_general(
            (blocks // 16).astype(jnp.float32), hits, (((1,), (1,)), ((), ())), preferred_element_type=jnp.float32
        ) * 16.0 + lax.dot_general(
            (blocks % 16).astype(jnp.float32), hits, (((1,), (1,)), ((), ())), preferred_element_type=jnp.float32
        )
        line = jnp.concatenate(
            [listed, jnp.zeros((1, META - count), jnp.float32)], axis=1
        ).astype(jnp.int32)
        line = jnp.where(lane == count, n_full.astype(jnp.int32), line)
        line = jnp.where(lane == count + 1, (n_full + n_edge).astype(jnp.int32), line)
        line = jnp.where(lane == count + 2, start, line)
        line = jnp.where(lane == count + 3, me, line)
        outs[j][...] = line


def make_lists(rows, turns, flags, me, span_offset, owners, held, tokens):
    smem = pl.BlockSpec(memory_space=pltpu.SMEM)
    vmem = pl.BlockSpec(memory_space=pltpu.VMEM)
    return pl.pallas_call(
        functools.partial(list_kernel, owners, held, tokens, turns, flags),
        out_shape=[jax.ShapeDtypeStruct((1, META), jnp.int32)] * len(turns),
        in_specs=[smem, smem] + [vmem] * len(rows),
        out_specs=[vmem] * len(turns),
        cost_estimate=pl.CostEstimate(flops=1, bytes_accessed=1, transcendentals=0),
    )(me.reshape(1), span_offset, *rows)


def body(queries, latent, selection, span_offset, w_absorb, w_value, w_out):
    owners = lax.axis_size("ctx")
    groups = lax.axis_size("head")
    me = lax.axis_index("ctx")
    column = lax.axis_index("head")
    chips = owners // 2
    depth = 3 * selection.shape[1] // (2 * owners)
    heads = w_absorb.shape[0]
    tokens = queries.shape[0]
    sibling = [(i, i ^ 1) for i in range(owners)]
    turns = range(1, chips)
    ahead = {t: [(i, (i + 2 * t) % owners) for i in range(owners)] for t in turns}
    back = {t: [(i, (i - 2 * t) % owners) for i in range(owners)] for t in turns}
    own = latent.T

    held = latent.shape[0] // BT

    far_queries = {t: lax.ppermute(queries, "ctx", ahead[t]) for t in turns}
    sib = lax.ppermute(own, "ctx", sibling)
    far_rows = {t: lax.ppermute(selection, "ctx", ahead[t]) for t in turns}
    lists = functools.partial(
        make_lists, me=me, span_offset=span_offset, owners=owners, held=held, tokens=tokens
    )
    near_meta, side_meta, *far_metas = lists(
        [selection, selection] + [far_rows[t] for t in turns],
        [0, 0, *turns],
        [(True, False), (False, True)] + [(True, True)] * (chips - 1),
    )
    weights = (w_absorb, w_value)
    whole = [(0, tokens)]
    (near,) = attend(near_meta, queries, own, own, *weights, depth, 1024, whole)
    (near,) = attend(side_meta, queries, own, sib, *weights, depth, 1024, whole, near)
    cuts = [(0, FIRST), (FIRST, tokens)] if chips == 2 else whole
    if chips == 2:
        far_near = lax.ppermute(near, "ctx", ahead[1])
        meta, near = lax.optimization_barrier((far_metas[0], near))
        fars = attend(meta, far_queries[1], own, sib, *weights, 2 * depth, 1024, cuts)
        *fars, far_near = lax.optimization_barrier((*fars, far_near))
        gots = []
        for far in fars:
            if gots:
                far, gots[-1] = lax.optimization_barrier((far, gots[-1]))
            gots.append(lax.ppermute(far, "ctx", ahead[1]))

        def mine_of(c, last):
            got, *_ = lax.optimization_barrier((gots[c], *last))
            return settle(near, far_near, fars[c], got, cuts[c][0], heads)
    else:
        arrived = [near]
        for t in turns:
            (far,) = attend(far_metas[t - 1], far_queries[t], own, sib, *weights, 2 * depth, 1024, whole)
            arrived.append(lax.ppermute(far, "ctx", back[t]))
        mine = combine(arrived, heads)
        mine = jnp.concatenate([mine] + [lax.ppermute(mine, "ctx", ahead[t]) for t in turns], axis=0)

        def mine_of(c, last):
            return mine

    outputs, last = [], []
    for c, (low, high) in enumerate(cuts):
        piece = high - low
        mine = mine_of(c, last)
        shares = project(mine, lax.ppermute(mine, "ctx", sibling), w_out)

        def share_of(block):
            turn = (me // 2 - block // 2) % chips
            place = (me + block) % 2 * chips + turn
            return lax.dynamic_slice_in_dim(shares, place * piece, piece, 0)

        steps = sorted(range(1, groups), key=lambda s: min(s, groups - s))
        moved = [
            lax.ppermute(
                share_of((column + s) % groups), "head", [(i, (i + s) % groups) for i in range(groups)]
            )
            for s in steps
        ]
        last = [shares]
        arrived = [share_of(column)] + moved
        outputs.append(sum(a.astype(jnp.float32) for a in arrived).astype(jnp.bfloat16))
    return jnp.concatenate(outputs, axis=0)


def solution(mesh):
    placed = (
        P(("groups", "ctx"), "head"),
        P(("groups", "ctx"), None),
        P(("groups", "ctx"), None),
        P("groups"),
        P("head", None, None),
        P("head", None, None),
        P("head", "ctx"),
    )
    return jax.shard_map(
        body, mesh=mesh, in_specs=placed, out_specs=P(("groups", "head"), "ctx"), check_vma=False
    )
```
